256 devices in a mesh: row: 16 (over y_lo, x, core), col: 16 (over y_hi, z).
Axes of the slice: x: 4, y: 4 (y_hi: 2, y_lo: 2; y = y_hi * 2 + y_lo), z: 8, core: 2. Of those that a mesh axis runs over, the one named last changes fastest.
Arguments:
- query: bfloat16 [2, 96, 1024, 128], P(None, 'row', 'col'), may hold values from -6 to 6
- key: bfloat16 [2, 96, 1024, 128], P(None, 'row', 'col'), may hold values from -6 to 6
- value: bfloat16 [2, 96, 1024, 128], P(None, 'row', 'col'), may hold values from -6 to 6
- grad_out: bfloat16 [2, 96, 1024, 128], P(None, 'row', 'col'), may hold values from -1.5 to 1.5
- pair_bias: bfloat16 [2, 4, 1024, 1024], P(None, None, 'col'), may hold values from -6 to 250
- crop_lengths: int32 [2], replicated, may hold values from 256 to 1024, as said below
Outputs:
- grad_query: float32 [2, 96, 1024, 128], P(None, 'row', 'col')
- grad_key: float32 [2, 96, 1024, 128], P(None, 'row', 'col')
- grad_value: float32 [2, 96, 1024, 128], P(None, 'row', 'col')
- grad_bias: float32 [2, 4, 1024, 1024], P(None, None, 'col', 'row')
The draws below stay inside these ranges and needn't reach their ends.
Inputs may be any that keep to these rules, and one draw needn't show every extreme that they name: `crop_lengths`: every crop has at least 256 valid residues, and some crop has all 1024.
All inputs are finite; a program needn't handle non-finite values.
Results may differ from the reference program's by a relative error of at most 0.0031.
Values may be sent and summed in bfloat16 or wider, within the bound.
A program may use at most 128 MiB of HBM per device.

```python
import jax
import jax.numpy as jnp
from jax import lax

H = 4
HD = 32
SEQ = 1024
CROPS = 2
ROWS = 96


def draw_pair_bias(key, part):
    key = jax.random.fold_in(key, 11)
    keys = jax.random.split(key, 1)
    full_shape = (CROPS, H, SEQ, SEQ)
    base = jnp.clip(jax.random.normal(keys[0], full_shape, jnp.float32), -6.0, 6.0)
    return base.astype(jnp.bfloat16)


def draw_crop_lengths(key, part):
    key = jax.random.fold_in(key, 5)
    keys = jax.random.split(key, 2)
    drawn = jax.random.randint(keys[0], (CROPS,), SEQ // 4, SEQ + 1)
    full_crop = jax.random.randint(keys[1], (), 0, CROPS)
    return jnp.where(lax.iota(jnp.int32, CROPS) == full_crop, SEQ, drawn).astype(jnp.int32)


def levels(rng, shape, cuts, least, high):
    factor_of = 1.0
    for dim, parts in cuts:
        heights = jax.random.uniform(jax.random.fold_in(jax.random.fold_in(rng, 6), dim), (parts,), jnp.float32, least / len(cuts), high / len(cuts))
        factor_of = factor_of * jnp.repeat(jnp.exp(heights), shape[dim] // parts).reshape((-1,) + (1,) * (len(shape) - 1 - dim))
    return factor_of


def normal_values(rng, extent, spread, reach, cuts=(), held_as=jnp.bfloat16):
    values = spread * jax.random.normal(rng, extent, jnp.float32)
    if cuts:
        values = values * levels(rng, extent, cuts, -0.22, 0.18)
    return jnp.clip(values, -reach, reach).astype(held_as)


def setup_inputs(seed: int = 0) -> dict:
    seeds = jax.random.split(jax.random.key(seed), 7)
    query = normal_values(seeds[0], (CROPS, ROWS, SEQ, H * HD), 1.0, 6.0, ((1, 16), (2, 16)))
    key = normal_values(seeds[1], (CROPS, ROWS, SEQ, H * HD), 1.0, 6.0, ((1, 16), (2, 16)))
    value = normal_values(seeds[2], (CROPS, ROWS, SEQ, H * HD), 1.0, 6.0, ((1, 16), (2, 16)))
    grad_out = normal_values(seeds[3], (CROPS, ROWS, SEQ, H * HD), 0.25, 1.5, ((1, 16), (2, 16)))
    pair_bias = draw_pair_bias(jax.random.fold_in(seeds[6], 71), 0)
    crop_lengths = draw_crop_lengths(jax.random.fold_in(seeds[6], 71), 0)
    return dict(query=query, key=key, value=value, grad_out=grad_out, pair_bias=pair_bias, crop_lengths=crop_lengths)


def row_grads(query_row, key_row, value_row, grad_row, bias_crop, length):
    scale = HD ** -0.5
    query_heads = query_row.astype(jnp.float32).reshape(SEQ, H, HD)
    key_heads = key_row.astype(jnp.float32).reshape(SEQ, H, HD)
    value_heads = value_row.astype(jnp.float32).reshape(SEQ, H, HD)
    grad_heads = grad_row.astype(jnp.float32).reshape(SEQ, H, HD)
    scores = jnp.einsum('jhd,khd->hjk', query_heads, key_heads) * scale + bias_crop.astype(jnp.float32)
    key_valid = (jnp.arange(SEQ, dtype=jnp.int32) < length)[None, None, :]
    scores = jnp.where(key_valid, scores, -1e30)
    log_total = jax.nn.logsumexp(scores, axis=-1, keepdims=True)
    probs = jnp.where(key_valid, jnp.exp(scores - log_total), 0.0)
    dprobs = jnp.einsum('jhd,khd->hjk', grad_heads, value_heads)
    delta = jnp.sum(probs * dprobs, axis=-1, keepdims=True)
    probs_half = lax.optimization_barrier(probs.astype(jnp.bfloat16)).astype(jnp.float32)
    grad_value = jnp.einsum('hjk,jhd->khd', probs_half, grad_heads)
    dscores = probs * (dprobs - delta)
    dscores_half = lax.optimization_barrier(dscores.astype(jnp.bfloat16)).astype(jnp.float32)
    grad_query = scale * jnp.einsum('hjk,khd->jhd', dscores_half, key_heads)
    grad_key = scale * jnp.einsum('hjk,jhd->khd', dscores_half, query_heads)
    return (grad_query.reshape(SEQ, H * HD), grad_key.reshape(SEQ, H * HD),
            grad_value.reshape(SEQ, H * HD), dscores)


def reference(query, key, value, grad_out, pair_bias, crop_lengths):
    query_list, key_list, value_list, bias_list = [], [], [], []
    for crop_index in range(CROPS):
        bias_crop = pair_bias[crop_index]
        length = crop_lengths[crop_index]

        def one_row(total, inputs):
            query_row, key_row, value_row, grad_row = inputs
            grad_query, grad_key, grad_value, dscores = row_grads(query_row, key_row, value_row, grad_row, bias_crop, length)
            return total + dscores, (grad_query, grad_key, grad_value)

        start_total = jnp.zeros((H, SEQ, SEQ), jnp.float32)
        total, stacked = lax.scan(one_row, start_total, (query[crop_index], key[crop_index], value[crop_index], grad_out[crop_index]))
        query_list.append(stacked[0])
        key_list.append(stacked[1])
        value_list.append(stacked[2])
        bias_list.append(total)
    return (jnp.stack(query_list), jnp.stack(key_list), jnp.stack(value_list), jnp.stack(bias_list))
```

```python
import functools
import jax, jax.numpy as jnp
from jax import lax
from jax.sharding import PartitionSpec as P
from jax.experimental import pallas as pl
from jax.experimental.pallas import tpu as pltpu
HD=32; SEQ=1024; NP=3
LOG2E=1.4426950408889634
SCALE=HD**-0.5
B=256
R=16

def nt(a,b): return lax.dot_general(a,b,(((1,),(1,)),((),())),preferred_element_type=jnp.float32)
def nn(a,b): return lax.dot_general(a,b,(((1,),(0,)),((),())),preferred_element_type=jnp.float32)

def prep(p, t_ref, tt, tq, td, kr):
    lane = lax.broadcasted_iota(jnp.int32,(SEQ,128),1)
    x = t_ref[p]
    tt[p] = x.T
    zero = jnp.zeros_like(x)
    tq[p] = jnp.where(lane<HD, x, zero)
    td[p] = jnp.where((lane>=HD)&(lane<2*HD), x, zero)
    y = pltpu.roll(x.astype(jnp.float32), 64, 1).astype(jnp.bfloat16)
    kr[p] = jnp.where(lane<HD, y, zero)

def kernel(len_ref, t_ref, bias_ref, g_ref, db_ref, tt, tq, td, kr, s_ref, dp_ref, b2_ref, ph, dsh, dkt, dvt, dq):
    n = len_ref[0]
    for p in range(NP):
        prep(p, t_ref, tt, tq, td, kr)
    dkt[...] = jnp.zeros_like(dkt); dvt[...] = jnp.zeros_like(dvt)
    def jblock(jb, _):
        j0 = pl.multiple_of(jb*B, B)
        rows = pl.ds(j0, B)
        for p in range(NP):
            rt = jnp.concatenate([tt[p,64:128],tt[p,0:64]],axis=0)
            s_ref[p%2] = nn(tq[p,rows,:], rt)
            dp_ref[p%2] = nn(td[p,rows,:], rt)
            for c in range(B//R):
                r = pl.ds(c*R,R)
                jr = pl.ds(j0+c*R,R)
                if p==0:
                    col = lax.broadcasted_iota(jnp.int32,(R,SEQ),1)
                    b2 = jnp.where(col<n, bias_ref[jr,:].astype(jnp.float32)*LOG2E, -1e30)
                    b2_ref[r,:] = b2
                else:
                    b2 = b2_ref[r,:]
                s = s_ref[p%2,r,:]*(SCALE*LOG2E)+b2
                m = jnp.max(s,axis=1,keepdims=True)
                e = jnp.exp2(s-m)
                dp = dp_ref[p%2,r,:]
                l = jnp.sum(e,axis=1,keepdims=True)
                w = jnp.sum(e*dp,axis=1,keepdims=True)
                rl = 1.0/l
                pr = e*rl
                ds = pr*(dp-w*rl)
                ph[p%2,r,:] = pr.astype(jnp.bfloat16)
                dsh[p%2,r,:] = ds.astype(jnp.bfloat16)
                if p==0: db_ref[jr,:] = ds
                else: db_ref[jr,:] += ds
            dsv = dsh[p%2]
            dq[p,rows,:] = nn(dsv, kr[p])
            dkt[p] += nn(tt[p,0:32,rows], dsv)
            dvt[p] += nn(tt[p,32:64,rows], ph[p%2])
        return 0
    lax.fori_loop(0, SEQ//B, jblock, 0)
    for p in range(NP):
        z = jnp.zeros((HD,SEQ),jnp.float32)
        acc = jnp.concatenate([z,dkt[p]*SCALE,dvt[p],z],axis=0)
        g_ref[p] = (acc.T + dq[p]*SCALE).astype(jnp.bfloat16)

def attn(n, t, bias):
    V=pltpu.VMEM; bf=jnp.bfloat16; f=jnp.float32
    return pl.pallas_call(kernel,
      out_shape=(jax.ShapeDtypeStruct((NP,SEQ,128),bf), jax.ShapeDtypeStruct((SEQ,SEQ),f)),
      in_specs=[pl.BlockSpec(memory_space=pltpu.SMEM),pl.BlockSpec(memory_space=V),pl.BlockSpec(memory_space=V)],
      out_specs=(pl.BlockSpec(memory_space=V),pl.BlockSpec(memory_space=V)),
      scratch_shapes=[V((NP,128,SEQ),bf),V((NP,SEQ,128),bf),V((NP,SEQ,128),bf),V((NP,SEQ,128),bf),
        V((2,B,SEQ),f),V((2,B,SEQ),f),V((B,SEQ),f),V((2,B,SEQ),bf),V((2,B,SEQ),bf),
        V((NP,HD,SEQ),f),V((NP,HD,SEQ),f),V((NP,SEQ,128),f)],
      compiler_params=pltpu.CompilerParams(vmem_limit_bytes=60*2**20),
    )(n,t,bias)


def per_device(query, key, value, grad_out, pair_bias, crop_lengths):
    me_col = lax.axis_index("col")
    me_row = lax.axis_index("row")
    def heads(x):
        return x.reshape(2, 2, 3, 64, 4, HD)
    t = jnp.concatenate([heads(query), heads(grad_out), heads(key), heads(value)], axis=-1)
    t = t.transpose(0, 4, 1, 2, 3, 5).reshape(16, 3, 64, 128)
    t = lax.all_to_all(t, "col", 0, 0, tiled=False)
    t = t.transpose(1, 0, 2, 3).reshape(3, SEQ, 128)
    part = lax.dynamic_slice_in_dim(pair_bias, me_row * 4, 4, 2).reshape(8, 1, 4, SEQ)
    part = jnp.broadcast_to(part, (8, 2, 4, SEQ)).reshape(16, 4, SEQ)
    part = lax.all_to_all(part, "col", 0, 0, tiled=False)
    bias = lax.all_gather(part, "row", axis=1, tiled=True).reshape(SEQ, SEQ)
    n = lax.dynamic_slice(crop_lengths, (me_col // 8,), (1,))
    g, db = attn(n, t, bias)
    g = g.reshape(3, 16, 64, 128).transpose(1, 0, 2, 3)
    g = lax.all_to_all(g, "col", 0, 0, tiled=False)
    g = g.reshape(2, 4, 2, 3, 64, 4, HD).transpose(5, 0, 2, 3, 4, 1, 6).reshape(4, 2, 6, 64, 128).astype(jnp.float32)
    db = lax.psum_scatter(db, "row", scatter_dimension=1, tiled=True).reshape(16, 64, 64)
    db = lax.all_to_all(db, "col", 0, 0, tiled=False)
    db = db.reshape(2, 4, 2, 64, 64).sum(2)
    return g[0], g[1], g[2], db


def solution(mesh):
    spec = P(None, "row", "col", None)
    return jax.shard_map(
        per_device,
        mesh=mesh,
        in_specs=(spec, spec, spec, spec, P(None, None, "col", None), P()),
        out_specs=(spec, spec, spec, P(None, None, "col", "row")),
        check_vma=False,
    )
```

```python
import functools

import jax
import jax.numpy as jnp
from jax import lax
from jax.experimental import pallas as pl
from jax.experimental.pallas import tpu as pltpu
from jax.sharding import PartitionSpec as P

H = 4
HD = 32
SEQ = 1024
NCOL = 16
BLK = SEQ // NCOL
NP = 3
NCHIP = 8
B = 256
NJ = SEQ // B
R = 16
HALF = B // 2
LOG2E = 1.4426950408889634
SCALE = HD**-0.5
F32 = jnp.float32
BF16 = jnp.bfloat16


def nn(a, b):
    return lax.dot_general(a, b, (((1,), (0,)), ((), ())), preferred_element_type=F32)


def wait_for(ref, sem):
    pltpu.make_async_copy(ref, ref, sem).wait()


def send(src, dst, send_sem, recv_sem, where):
    pltpu.make_async_remote_copy(
        src_ref=src,
        dst_ref=dst,
        send_sem=send_sem,
        recv_sem=recv_sem,
        device_id=where,
        device_id_type=pl.DeviceIdType.MESH,
    ).start()


def kernel(
    len_ref, q_ref, k_ref, v_ref, g_ref, bias_ref,
    dq_out, dk_out, dv_out, db_out,
    tsend, tall, bias_full, b2, tt, tq, td, kr, s_ref, dp_ref, ph, dsh, dkt, dvt, dq,
    gsend, gin, db, sib, rsend, red, fsend, fin, last, lastin,
    t_ss, t_rs, b1_ss, b1_rs, b1_ls, b2_ss, b2_rs, b3_ss, b3_rs, g_ss, g_rs,
    a_ss, a_rs, r_ss, r_rs, f_ss, f_rs, l_ss, l_rs,
):
    row = lax.axis_index("row")
    me = lax.axis_index("col")
    chip = row // 2
    core = row % 2
    sibling = {"row": row + 1 - 2 * core}

    def peer(o):
        return lax.rem(me + o, NCOL)

    def row_peer(o):
        return lax.rem(chip + o, NCHIP)

    barrier = pltpu.get_barrier_semaphore()
    for o in range(1, NCOL):
        pl.semaphore_signal(barrier, inc=1, device_id={"col": peer(o)}, device_id_type=pl.DeviceIdType.MESH)
    for o in range(1, NCHIP):
        pl.semaphore_signal(barrier, inc=1, device_id={"row": 2 * row_peer(o) + core}, device_id_type=pl.DeviceIdType.MESH)
    pl.semaphore_signal(barrier, inc=1, device_id=sibling, device_id_type=pl.DeviceIdType.MESH)

    block_of = lax.broadcasted_iota(jnp.int32, (BLK, 128), 1) // HD

    def pack(p):
        for c in range(2):
            for half in range(2):
                i = half * 3 + p
                arrays = [x[c, i].astype(F32) for x in (q_ref, g_ref, k_ref, v_ref)]
                for h in range(H):
                    out = None
                    for a in range(4):
                        d = (a - h) % 4
                        x = arrays[a] if d == 0 else pltpu.roll(arrays[a], d * HD, 1)
                        out = x if out is None else jnp.where(block_of == a, x, out)
                    tsend[p, c * 8 + h * 2 + half] = out.astype(BF16)
        tall[p, pl.ds(pl.multiple_of(me * BLK, BLK), BLK), :] = tsend[p, me]

    def send_pack(p):
        for o in range(1, NCOL):
            to = peer(o)
            send(
                tsend.at[p, to],
                tall.at[p, pl.ds(pl.multiple_of(me * BLK, BLK), BLK)],
                t_ss.at[p],
                t_rs.at[p],
                {"col": to},
            )

    pack(0)
    pl.semaphore_wait(barrier, NCOL - 1 + NCHIP - 1 + 1)

    my_rows = pl.ds(pl.multiple_of(core * 32 + (chip // 4) * 16, 16), 16)
    my_lanes = pl.ds(pl.multiple_of((chip % 4) * 256, 256), 256)
    for o in range(1, NCOL):
        to = peer(o)
        send(
            bias_ref.at[to // 8, (to // 2) % 4, my_rows, my_lanes],
            bias_full.at[me, my_rows, my_lanes],
            b1_ss,
            b1_rs,
            {"col": to},
        )
    own = pltpu.make_async_copy(
        bias_ref.at[me // 8, (me // 2) % 4, my_rows, my_lanes],
        bias_full.at[me, my_rows, my_lanes],
        b1_ls,
    )
    own.start()
    send_pack(0)
    pack(1)
    send_pack(1)
    pack(2)
    send_pack(2)
    own.wait()
    wait_for(bias_full.at[pl.ds(0, NCOL - 1), pl.ds(0, 16), pl.ds(0, 256)], b1_rs)
    for jb in range(NJ):
        mine = bias_full.at[pl.ds(jb * 4, 4), my_rows, my_lanes]
        for o in range(1, NCHIP):
            send(mine, mine, b2_ss.at[jb], b2_rs.at[jb], {"row": 2 * row_peer(o) + core})

    def bias_to_sibling(jb):
        wait_for(bias_full.at[pl.ds(0, 7), pl.ds(0, 64), pl.ds(0, 256)], b2_rs.at[jb])
        half = bias_full.at[pl.ds(jb * 4, 4), pl.ds(pl.multiple_of(core * 32, 32), 32)]
        send(half, half, b3_ss.at[jb], b3_rs.at[jb], sibling)

    bias_to_sibling(0)
    n = len_ref[me // 8]
    dkt[...] = jnp.zeros_like(dkt)
    dvt[...] = jnp.zeros_like(dvt)

    def prep(p):
        wait_for(tall.at[p, pl.ds(0, BLK * (NCOL - 1))], t_rs.at[p])
        lane = lax.broadcasted_iota(jnp.int32, (SEQ, 128), 1)
        x = tall[p]
        xt = x.T
        tt[pl.ds(0, 64), :] = xt[64:128]
        tt[pl.ds(64, 64), :] = xt[0:64]
        zero = jnp.zeros_like(x)
        tq[...] = jnp.where(lane < HD, x, zero)
        td[...] = jnp.where((lane >= HD) & (lane < 2 * HD), x, zero)
        y = pltpu.roll(x.astype(F32), 64, 1).astype(BF16)
        kr[...] = jnp.where(lane < HD, y, zero)

    def mask_bias(jb):
        col = lax.broadcasted_iota(jnp.int32, (R, SEQ), 1)
        for c in range(B // R):
            x = bias_full[jb * 4 + c // 4, pl.ds((c % 4) * R, R), :].astype(F32)
            b2[pl.ds(pl.multiple_of(jb * B + c * R, R), R), :] = jnp.where(col < n, x * LOG2E, -1e30)

    def tile(p, jb, first):
        j0 = pl.multiple_of(jb * B, B)
        rows = pl.ds(j0, B)
        rt = tt[...]
        s_ref[...] = nn(tq[rows, :], rt)
        dp_ref[...] = nn(td[rows, :], rt)
        for c in range(B // R):
            r = pl.ds(c * R, R)
            jr = pl.ds(pl.multiple_of(j0 + c * R, R), R)
            s = s_ref[r, :] * (SCALE * LOG2E) + b2[jr, :]
            m = jnp.max(s, axis=1, keepdims=True)
            e = jnp.exp2(s - m)
            dp = dp_ref[r, :]
            rl = 1.0 / jnp.sum(e, axis=1, keepdims=True)
            w = jnp.sum(e * dp, axis=1, keepdims=True)
            pr = e * rl
            ds = pr * (dp - w * rl)
            ph[r, :] = pr.astype(BF16)
            dsh[r, :] = ds.astype(BF16)
            db[jr, :] += ds
        dsv = dsh[...]
        dq[rows, :] = nn(dsv, kr[...])
        dkt[...] += nn(tt[pl.ds(64, 32), rows], dsv)
        dvt[...] += nn(tt[pl.ds(96, 32), rows], ph[...])

    def finish(p):
        z = jnp.zeros((HD, SEQ), F32)
        acc = jnp.concatenate([z, dkt[...] * SCALE, dvt[...], z], axis=0)
        gsend[p] = (acc.T + dq[...] * SCALE).astype(BF16)
        dkt[...] = jnp.zeros_like(dkt)
        dvt[...] = jnp.zeros_like(dvt)
        mine = pl.ds(pl.multiple_of(me * BLK, BLK), BLK)
        gin[p, me] = gsend[p, mine, :]
        for o in range(1, NCOL):
            to = peer(o)
            send(
                gsend.at[p, pl.ds(pl.multiple_of(to * BLK, BLK), BLK)],
                gin.at[p, me],
                g_ss.at[p],
                g_rs.at[p],
                {"col": to},
            )

    def db_to_sibling(jb):
        theirs = db.at[pl.ds(pl.multiple_of(jb * B + (1 - core) * HALF, HALF), HALF)]
        send(theirs, sib.at[jb], a_ss.at[jb], a_rs.at[jb], sibling)

    def db_over_row(jb):
        wait_for(sib.at[jb], a_rs.at[jb])
        for o in range(NCHIP):
            x = (
                db[pl.ds(pl.multiple_of(jb * B + core * HALF, HALF), HALF), pl.ds(o * 128, 128)]
                + sib[jb, :, pl.ds(o * 128, 128)]
            )
            rsend[jb, o] = x.astype(BF16)
        red[jb, chip] = rsend[jb, chip]
        for o in range(1, NCHIP):
            to = row_peer(o)
            send(rsend.at[jb, to], red.at[jb, chip], r_ss.at[jb], r_rs.at[jb], {"row": 2 * to + core})

    def db_to_owner(jb):
        wait_for(red.at[jb, pl.ds(0, NCHIP - 1)], r_rs.at[jb])
        total = red[jb, 0].astype(F32)
        for o in range(1, NCHIP):
            total = total + red[jb, o].astype(F32)
        for e in range(2):
            to = jb * 4 + core * 2 + e
            part = total[e * BLK : (e + 1) * BLK]
            fsend[jb * 2 + e] = part

            @pl.when(to == me)
            def _():
                fin[me] = part

            @pl.when(to != me)
            def _():
                send(fsend.at[jb * 2 + e], fin.at[me], f_ss, f_rs, {"col": to})

    @pl.loop(0, NP * NJ)
    def _(it):
        p = it // NJ
        jb = it % NJ

        @pl.when(jb == 0)
        def _():
            prep(p)

        @pl.when(p == 0)
        def _():
            @pl.when(jb < NJ - 1)
            def _():
                bias_to_sibling(jb + 1)

            wait_for(bias_full.at[pl.ds(0, 4), pl.ds(0, 32)], b3_rs.at[jb])
            mask_bias(jb)

            db[pl.ds(pl.multiple_of(jb * B, B), B), :] = jnp.zeros((B, SEQ), F32)

        tile(p, jb, None)

        @pl.when(p == NP - 1)
        def _():
            db_to_sibling(jb)

        @pl.when(jb == NJ - 1)
        def _():
            finish(p)

        @pl.when((p == NP - 1) & (jb >= 1))
        def _():
            db_over_row(jb - 1)

        @pl.when((p == NP - 1) & (jb >= 2))
        def _():
            db_to_owner(jb - 2)

    db_over_row(NJ - 1)
    db_to_owner(NJ - 2)

    def unpack(p):
        wait_for(gin.at[p, pl.ds(0, NCOL - 1)], g_rs.at[p])
        for c in range(2):
            for half in range(2):
                i = half * 3 + p
                parts = [gin[p, c * 8 + h * 2 + half].astype(F32) for h in range(H)]
                for a, out_ref in enumerate((dq_out, dk_out, dv_out)):
                    out = None
                    for h in range(H):
                        d = (h - a) % 4
                        x = parts[h] if d == 0 else pltpu.roll(parts[h], d * HD, 1)
                        out = x if out is None else jnp.where(block_of == h, x, out)
                    out_ref[c, i] = out

    unpack(0)
    db_to_owner(NJ - 1)
    unpack(1)
    owner = (me // 2) % 2 == core

    def put(value):
        x = jnp.where(core == 0, value, pltpu.roll(value, 64, 1))
        return x[:, 0:64]

    @pl.when(owner)
    def _():
        wait_for(fin.at[pl.ds(0, NCOL - 1)], f_rs)
        for e in range(8):
            x = fin[2 * e] + fin[2 * e + 1]
            last[e] = x
            db_out[e // 4, e % 4] = put(x)
        send(last, lastin, l_ss, l_rs, sibling)

    unpack(2)

    @pl.when(owner)
    def _():
        wait_for(last, l_ss)
        wait_for(fsend.at[pl.ds(0, 7)], f_ss)

    @pl.when(jnp.logical_not(owner))
    def _():
        wait_for(lastin, l_rs)
        for e in range(8):
            db_out[e // 4, e % 4] = put(lastin[e])
        wait_for(fsend, f_ss)

    wait_for(bias_full.at[pl.ds(0, NCOL - 1), pl.ds(0, 16), pl.ds(0, 256)], b1_ss)
    for p in range(NP):
        wait_for(tall.at[p, pl.ds(0, BLK * (NCOL - 1))], t_ss.at[p])
        wait_for(gin.at[p, pl.ds(0, NCOL - 1)], g_ss.at[p])
    for jb in range(NJ):
        wait_for(bias_full.at[pl.ds(0, 7), pl.ds(0, 64), pl.ds(0, 256)], b2_ss.at[jb])
        wait_for(bias_full.at[pl.ds(0, 4), pl.ds(0, 32)], b3_ss.at[jb])
        wait_for(sib.at[jb], a_ss.at[jb])
        wait_for(red.at[jb, pl.ds(0, NCHIP - 1)], r_ss.at[jb])


def per_device(query, key, value, grad_out, pair_bias, crop_lengths):
    V = pltpu.VMEM
    D = pltpu.SemaphoreType.DMA
    grad = jax.ShapeDtypeStruct(query.shape, F32)
    vm = pl.BlockSpec(memory_space=V)
    return pl.pallas_call(
        kernel,
        out_shape=(grad, grad, grad, jax.ShapeDtypeStruct((2, H, BLK, BLK), F32)),
        in_specs=[pl.BlockSpec(memory_space=pltpu.SMEM)] + [vm] * 5,
        out_specs=(vm,) * 4,
        scratch_shapes=[
            V((NP, NCOL, BLK, 128), BF16),
            V((NP, SEQ, 128), BF16),
            V((NCOL, BLK, SEQ), BF16),
            V((SEQ, SEQ), F32),
            V((128, SEQ), BF16),
            V((SEQ, 128), BF16),
            V((SEQ, 128), BF16),
            V((SEQ, 128), BF16),
            V((B, SEQ), F32),
            V((B, SEQ), F32),
            V((B, SEQ), BF16),
            V((B, SEQ), BF16),
            V((HD, SEQ), F32),
            V((HD, SEQ), F32),
            V((SEQ, 128), F32),
            V((NP, SEQ, 128), BF16),
            V((NP, NCOL, BLK, 128), BF16),
            V((SEQ, SEQ), F32),
            V((NJ, HALF, SEQ), F32),
            V((NJ, NCHIP, HALF, 128), BF16),
            V((NJ, NCHIP, HALF, 128), BF16),
            V((8, BLK, 128), F32),
            V((NCOL, BLK, 128), F32),
            V((8, BLK, 128), F32),
            V((8, BLK, 128), F32),
            D((NP,)), D((NP,)), D, D, D, D((NJ,)), D((NJ,)), D((NJ,)), D((NJ,)), D((NP,)), D((NP,)),
            D((NJ,)), D((NJ,)), D((NJ,)), D((NJ,)), D, D, D, D,
        ],
        compiler_params=pltpu.CompilerParams(
            vmem_limit_bytes=60 * 2**20, collective_id=0, has_side_effects=True
        ),
        cost_estimate=pl.CostEstimate(flops=8 * 10**9, bytes_accessed=4 * 10**6, transcendentals=3 * 2**20),
    )(crop_lengths, query, key, value, grad_out, pair_bias)


def solution(mesh):
    spec = P(None, "row", "col", None)
    return jax.shard_map(
        per_device,
        mesh=mesh,
        in_specs=(spec, spec, spec, spec, P(None, None, "col", None), P()),
        out_specs=(spec, spec, spec, P(None, None, "col", "row")),
        check_vma=False,
    )
```

```python
import jax
import jax.numpy as jnp
from jax import lax
from jax.experimental import pallas as pl
from jax.experimental.pallas import tpu as pltpu
from jax.sharding import PartitionSpec as P

H = 4
HD = 32
SEQ = 1024
NZ = 8
BLK = 64
HALF = SEQ // 2
NU = 3
NCHIP = 8
B = 256
NJ = HALF // B
R = 16
SUB = B // 2
LOG2E = 1.4426950408889634
SCALE = HD**-0.5
F32 = jnp.float32
BF16 = jnp.bfloat16
MESH = pl.DeviceIdType.MESH


def nn(a, b):
    return lax.dot_general(a, b, (((1,), (0,)), ((), ())), preferred_element_type=F32)


def wait_for(ref, sem):
    pltpu.make_async_copy(ref, ref, sem).wait()


def send(src, dst, send_sem, recv_sem, where):
    pltpu.make_async_remote_copy(
        src_ref=src,
        dst_ref=dst,
        send_sem=send_sem,
        recv_sem=recv_sem,
        device_id=where,
        device_id_type=MESH,
    ).start()


def at(index, size):
    return pl.ds(pl.multiple_of(index * size, size), size)


def kernel(
    len_ref, q_ref, k_ref, v_ref, g_ref, bias_ref,
    gq, gkv, fin,
    tsend, kv, qd, bias_full, b2, kvt, qdt, lhs, rhs, s_ref, dp_ref, ph, dsh, acc, dq, g32,
    psend, precv, gqsend, gkvsend, db, sib, rsend, red, fsend, own_fin,
    kv_ss, kv_rs, qd_ss, qd_rs, fw_ss, fw_rs, b1_ss, b1_rs, b1_ls, b2_ss, b2_rs, b3_ss, b3_rs,
    p_ss, p_rs, gq_ss, gq_rs, gk_ss, gk_rs, a_ss, a_rs, r_ss, r_rs, f_ss, f_rs, l_ss, l_rs,
):
    row = lax.axis_index("row")
    me = lax.axis_index("col")
    z = me % NZ
    yh = me // NZ
    chip = row // 2
    core = row % 2
    sibling = {"row": row + 1 - 2 * core}
    partner = {"col": (1 - yh) * NZ + z}
    others = [lax.rem(z + o, NZ) for o in range(1, NZ)]
    chips = [lax.rem(chip + o, NCHIP) for o in range(1, NCHIP)]

    def along_z(to):
        return {"col": yh * NZ + to}

    def along_row(to):
        return {"row": 2 * to + core}

    barrier = pltpu.get_barrier_semaphore()
    everyone = [along_z(to) for to in others] + [along_row(to) for to in chips] + [sibling, partner]
    for where in everyone:
        pl.semaphore_signal(barrier, inc=1, device_id=where, device_id_type=MESH)

    lane_block = lax.broadcasted_iota(jnp.int32, (BLK, 128), 1) // HD

    def lanes_from(parts):
        out = None
        for a, (x, b) in enumerate(parts):
            d = (a - b) % 4
            x = x if d == 0 else pltpu.roll(x, d * HD, 1)
            out = x if out is None else jnp.where(lane_block == a, x, out)
        return out

    def pack(u):
        for c in range(2):
            for kind, refs in enumerate(((k_ref, v_ref), (q_ref, g_ref))):
                arrays = [ref[c, 2 * u + e].astype(F32) for e in range(2) for ref in refs]
                for h in range(H):
                    tsend[u, kind, c * H + h] = lanes_from([(x, h) for x in arrays]).astype(BF16)
        kv[u, at(me, BLK), :] = tsend[u, 0, z]
        qd[u, at(z, BLK), :] = tsend[u, 1, z]

    def send_pack(u):
        for to in others:
            send(tsend.at[u, 0, to], kv.at[u, at(me, BLK)], kv_ss.at[u], kv_rs.at[u], along_z(to))
        for to in others:
            send(tsend.at[u, 1, to], qd.at[u, at(z, BLK)], qd_ss.at[u], qd_rs.at[u], along_z(to))

    def forward(u):
        wait_for(kv.at[u, pl.ds(0, BLK * (NZ - 1))], kv_rs.at[u])
        mine = kv.at[u, at(yh, HALF)]
        send(mine, mine, fw_ss.at[u], fw_rs.at[u], partner)

    my_rows = pl.ds(pl.multiple_of(core * 32 + (chip // 4) * 16, 16), 16)
    my_lanes = at(chip % 4, 256)

    def bias_to_chips(jb):
        mine = bias_full.at[pl.ds(jb * 4, 4), my_rows, my_lanes]
        for to in chips:
            send(mine, mine, b2_ss.at[jb], b2_rs.at[jb], along_row(to))

    def bias_to_sibling(jb):
        wait_for(bias_full.at[pl.ds(0, 7), :, pl.ds(0, 256)], b2_rs.at[jb])
        mine = bias_full.at[pl.ds(jb * 4, 4), at(core, 32)]
        send(mine, mine, b3_ss.at[jb], b3_rs.at[jb], sibling)

    pack(0)
    pl.semaphore_wait(barrier, len(everyone))
    for to in others:
        send(
            bias_ref.at[to // H, to % H, my_rows, my_lanes],
            bias_full.at[z, my_rows, my_lanes],
            b1_ss,
            b1_rs,
            along_z(to),
        )
    own = pltpu.make_async_copy(
        bias_ref.at[z // H, z % H, my_rows, my_lanes], bias_full.at[z, my_rows, my_lanes], b1_ls
    )
    own.start()
    send_pack(0)
    pack(1)
    own.wait()
    wait_for(bias_full.at[pl.ds(0, NZ - 1), pl.ds(0, 16), pl.ds(0, 256)], b1_rs)
    bias_to_chips(0)
    bias_to_chips(1)
    send_pack(1)
    forward(0)
    pack(2)
    send_pack(2)
    bias_to_sibling(0)
    n = len_ref[z // H]
    db[...] = jnp.zeros_like(db)

    def mask_bias(jb):
        col = lax.broadcasted_iota(jnp.int32, (R, SEQ), 1)
        for c in range(B // R):
            x = bias_full[jb * 4 + c // 4, pl.ds((c % 4) * R, R), :].astype(F32)
            b2[pl.ds(pl.multiple_of(jb * B + c * R, R), R), :] = jnp.where(col < n, x * LOG2E, -1e30)

    def prep(u):
        wait_for(qd.at[u, pl.ds(0, BLK * (NZ - 1))], qd_rs.at[u])
        x = qd[u]
        qdt[...] = x.T
        block = lax.broadcasted_iota(jnp.int32, x.shape, 1) // HD
        for b in range(4):
            lhs[b] = jnp.where(block == b, x, jnp.zeros_like(x))
        wait_for(kv.at[u, pl.ds(0, HALF)], fw_rs.at[u])
        x = kv[u]
        kvt[...] = x.T
        block = lax.broadcasted_iota(jnp.int32, x.shape, 1) // HD
        for e in range(2):
            rhs[e] = jnp.where(block == 2 * e, x, jnp.zeros_like(x))
        acc[...] = jnp.zeros_like(acc)
        dq[...] = jnp.zeros_like(dq)

    def tile(jb, e):
        j0 = pl.multiple_of(jb * B, B)
        rows = pl.ds(j0, B)
        keys = kvt[...]
        s_ref[...] = nn(lhs[2 * e, rows, :], keys)
        dp_ref[...] = nn(lhs[2 * e + 1, rows, :], keys)
        for c in range(B // R):
            r = pl.ds(c * R, R)
            jr = pl.ds(pl.multiple_of(j0 + c * R, R), R)
            s = s_ref[r, :] * (SCALE * LOG2E) + b2[jr, :]
            m = jnp.max(s, axis=1, keepdims=True)
            w = jnp.exp2(s - m)
            dp = dp_ref[r, :]
            rl = 1.0 / jnp.sum(w, axis=1, keepdims=True)
            delta = jnp.sum(w * dp, axis=1, keepdims=True) * rl
            pr = w * rl
            ds = pr * (dp - delta)
            ph[r, :] = pr.astype(BF16)
            dsh[r, :] = ds.astype(BF16)
            db[jr, :] += ds
        dsv = dsh[...]
        dq[rows, :] += nn(dsv, rhs[e])
        k_rows = pl.ds(pl.multiple_of(e * 64, 64), HD)
        v_rows = pl.ds(pl.multiple_of(e * 64 + HD, HD), HD)
        acc[k_rows, :] += nn(qdt[k_rows, rows], dsv)
        acc[v_rows, :] += nn(qdt[v_rows, rows], ph[...])

    def finish(u):
        even = (lax.broadcasted_iota(jnp.int32, (SEQ, 128), 1) // HD) % 2 == 0
        g = acc[...].T
        g32[...] = jnp.where(even, g * SCALE, g)
        psend[u] = g32[at(1 - yh, HALF), :].astype(BF16)
        send(psend.at[u], precv.at[u], p_ss.at[u], p_rs.at[u], partner)
        x = (dq[...] * SCALE).reshape(NZ, BLK, 128)
        even = (lax.broadcasted_iota(jnp.int32, (NZ, 32, 128), 2) // HD) % 2 == 0
        gqsend[u] = jnp.where(even, x[:, :32], pltpu.roll(x[:, 32:], HD, 2)).astype(BF16)
        gq[u, z] = gqsend[u, z]
        for to in others:
            send(gqsend.at[u, to], gq.at[u, z], gq_ss.at[u], gq_rs.at[u], along_z(to))

    def combine(u):
        wait_for(precv.at[u], p_rs.at[u])
        g = g32[at(yh, HALF), :] + precv[u].astype(F32)
        gkvsend[u] = g.astype(BF16).reshape(NZ, BLK, 128)
        gkv[u, z] = gkvsend[u, z]
        for to in others:
            send(gkvsend.at[u, to], gkv.at[u, z], gk_ss.at[u], gk_rs.at[u], along_z(to))

    def db_to_sibling(jb):
        theirs = db.at[pl.ds(pl.multiple_of(jb * B + (1 - core) * SUB, SUB), SUB)]
        send(theirs, sib.at[jb], a_ss.at[jb], a_rs.at[jb], sibling)

    def db_over_row(jb):
        wait_for(sib.at[jb], a_rs.at[jb])
        mine = pl.ds(pl.multiple_of(jb * B + core * SUB, SUB), SUB)
        for o in range(NCHIP):
            lanes = pl.ds(o * 128, 128)
            rsend[jb, o] = (db[mine, lanes] + sib[jb, :, lanes]).astype(BF16)
        red[jb, chip] = rsend[jb, chip]
        for to in chips:
            send(rsend.at[jb, to], red.at[jb, chip], r_ss.at[jb], r_rs.at[jb], along_row(to))

    def db_to_owner(jb):
        wait_for(red.at[jb, pl.ds(0, NCHIP - 1)], r_rs.at[jb])
        total = red[jb, 0].astype(F32)
        for o in range(1, NCHIP):
            total = total + red[jb, o].astype(F32)
        for e in range(2):
            to = jb * 4 + core * 2 + e
            fsend[jb * 2 + e] = total[e * BLK : (e + 1) * BLK]

            @pl.when(to == z)
            def _():
                fin[z] = fsend[jb * 2 + e]

            @pl.when(to != z)
            def _():
                send(fsend.at[jb * 2 + e], fin.at[z], f_ss, f_rs, along_z(to))

    @pl.loop(0, NU * 4)
    def _(it):
        u = it // 4
        jb = (it // 2) % 2
        e = it % 2

        @pl.when(it % 4 == 0)
        def _():
            prep(u)

        @pl.when((u == 0) & (e == 0))
        def _():
            wait_for(bias_full.at[pl.ds(0, 4), pl.ds(0, 32)], b3_rs.at[jb])
            mask_bias(jb)

        @pl.when(it == 1)
        def _():
            bias_to_sibling(1)

        @pl.when((it % 4 == 1) & (u < NU - 1))
        def _():
            forward(u + 1)

        @pl.when((it % 4 == 1) & (u > 0))
        def _():
            combine(u - 1)

        tile(jb, e)

        @pl.when((u == NU - 1) & (e == 1))
        def _():
            db_to_sibling(jb)

        @pl.when(it == NU * 4 - 2)
        def _():
            db_over_row(0)

        @pl.when(it % 4 == 3)
        def _():
            finish(u)

    db_over_row(1)
    db_to_owner(0)
    combine(NU - 1)
    db_to_owner(1)
    owner = (z // 2) % 2 == core

    @pl.when(owner)
    def _():
        wait_for(fin.at[pl.ds(0, NZ - 1)], f_rs)
        own_fin[...] = fin[...]
        send(own_fin, fin, l_ss, l_rs, sibling)
        wait_for(own_fin, l_ss)
        wait_for(fsend.at[pl.ds(0, 3)], f_ss)

    @pl.when(jnp.logical_not(owner))
    def _():
        wait_for(fin, l_rs)
        wait_for(fsend, f_ss)

    wait_for(bias_full.at[pl.ds(0, NZ - 1), pl.ds(0, 16), pl.ds(0, 256)], b1_ss)
    for u in range(NU):
        wait_for(gq.at[u, pl.ds(0, NZ - 1)], gq_rs.at[u])
        wait_for(gkv.at[u, pl.ds(0, NZ - 1)], gk_rs.at[u])
        wait_for(gq.at[u, pl.ds(0, NZ - 1)], gq_ss.at[u])
        wait_for(gkv.at[u, pl.ds(0, NZ - 1)], gk_ss.at[u])
        wait_for(kv.at[u, pl.ds(0, BLK * (NZ - 1))], kv_ss.at[u])
        wait_for(qd.at[u, pl.ds(0, BLK * (NZ - 1))], qd_ss.at[u])
        wait_for(kv.at[u, pl.ds(0, HALF)], fw_ss.at[u])
        wait_for(psend.at[u], p_ss.at[u])
    for jb in range(NJ):
        wait_for(bias_full.at[pl.ds(0, 7), :, pl.ds(0, 256)], b2_ss.at[jb])
        wait_for(bias_full.at[pl.ds(0, 4), pl.ds(0, 32)], b3_ss.at[jb])
        wait_for(sib.at[jb], a_ss.at[jb])
        wait_for(red.at[jb, pl.ds(0, NCHIP - 1)], r_ss.at[jb])


def unpack(core_ref, gq, gkv, fin, dq_out, dk_out, dv_out, db_out):
    lane_block = lax.broadcasted_iota(jnp.int32, (BLK, 128), 1) // HD

    def lanes_from(parts):
        out = None
        for h, (x, b) in enumerate(parts):
            d = (h - b) % 4
            x = x if d == 0 else pltpu.roll(x, d * HD, 1)
            out = x if out is None else jnp.where(lane_block == h, x, out)
        return out

    for u in range(NU):
        folded = [gq[u, h].astype(F32) for h in range(H)]
        folded = [jnp.concatenate([x, pltpu.roll(x, 128 - HD, 1)], axis=0) for x in folded]
        pairs = [gkv[u, h].astype(F32) for h in range(H)]
        for e in range(2):
            dq_out[0, 2 * u + e] = lanes_from([(x, 2 * e) for x in folded])
            dk_out[0, 2 * u + e] = lanes_from([(x, 2 * e) for x in pairs])
            dv_out[0, 2 * u + e] = lanes_from([(x, 2 * e + 1) for x in pairs])
    for h in range(H):
        x = fin[h]
        x = jnp.where(core_ref[0] == 0, x, pltpu.roll(x, 64, 1))
        db_out[0, h] = x[:, 0:64]


def per_device(query, key, value, grad_out, pair_bias, crop_lengths):
    V = pltpu.VMEM
    D = pltpu.SemaphoreType.DMA
    vm = pl.BlockSpec(memory_space=V)
    gq, gkv, fin = pl.pallas_call(
        kernel,
        out_shape=(
            jax.ShapeDtypeStruct((NU, NZ, 32, 128), BF16),
            jax.ShapeDtypeStruct((NU, NZ, BLK, 128), BF16),
            jax.ShapeDtypeStruct((NZ, BLK, 128), F32),
        ),
        in_specs=[pl.BlockSpec(memory_space=pltpu.SMEM)] + [vm] * 5,
        out_specs=(vm, vm, vm),
        scratch_shapes=[
            V((NU, 2, NZ, BLK, 128), BF16),
            V((NU, SEQ, 128), BF16),
            V((NU, HALF, 128), BF16),
            V((NZ, BLK, SEQ), BF16),
            V((HALF, SEQ), F32),
            V((128, SEQ), BF16),
            V((128, HALF), BF16),
            V((4, HALF, 128), BF16),
            V((2, SEQ, 128), BF16),
            V((B, SEQ), F32),
            V((B, SEQ), F32),
            V((B, SEQ), BF16),
            V((B, SEQ), BF16),
            V((128, SEQ), F32),
            V((HALF, 128), F32),
            V((SEQ, 128), F32),
            V((NU, HALF, 128), BF16),
            V((NU, HALF, 128), BF16),
            V((NU, NZ, 32, 128), BF16),
            V((NU, NZ, BLK, 128), BF16),
            V((HALF, SEQ), F32),
            V((NJ, SUB, SEQ), F32),
            V((NJ, NCHIP, SUB, 128), BF16),
            V((NJ, NCHIP, SUB, 128), BF16),
            V((4, BLK, 128), F32),
            V((NZ, BLK, 128), F32),
        ]
        + [D((NU,))] * 6
        + [D] * 3
        + [D((NJ,))] * 4
        + [D((NU,))] * 6
        + [D((NJ,))] * 4
        + [D] * 4,
        compiler_params=pltpu.CompilerParams(
            vmem_limit_bytes=60 * 2**20, collective_id=0, has_side_effects=True
        ),
        cost_estimate=pl.CostEstimate(flops=8 * 10**9, bytes_accessed=4 * 10**6, transcendentals=3 * 2**20),
    )(crop_lengths, query, key, value, grad_out, pair_bias)
    grad = jax.ShapeDtypeStruct(query.shape, F32)
    spec = pl.BlockSpec((1, 6, BLK, 128), lambda c: (c, 0, 0, 0))
    return pl.pallas_call(
        unpack,
        grid=(2,),
        out_shape=(grad, grad, grad, jax.ShapeDtypeStruct((2, H, BLK, BLK), F32)),
        in_specs=[
            pl.BlockSpec(memory_space=pltpu.SMEM),
            pl.BlockSpec((NU, H, 32, 128), lambda c: (0, c, 0, 0)),
            pl.BlockSpec((NU, H, BLK, 128), lambda c: (0, c, 0, 0)),
            pl.BlockSpec((H, BLK, 128), lambda c: (c, 0, 0)),
        ],
        out_specs=(spec, spec, spec, pl.BlockSpec((1, H, BLK, BLK), lambda c: (c, 0, 0, 0))),
    )(lax.rem(lax.axis_index("row"), 2)[None], gq, gkv, fin)


def solution(mesh):
    spec = P(None, "row", "col", None)
    return jax.shard_map(
        per_device,
        mesh=mesh,
        in_specs=(spec, spec, spec, spec, P(None, None, "col", None), P()),
        out_specs=(spec, spec, spec, P(None, None, "col", "row")),
        check_vma=False,
    )
```

```python
import jax
import jax.numpy as jnp
from jax import lax
from jax.experimental import pallas as pl
from jax.experimental.pallas import tpu as pltpu
from jax.sharding import PartitionSpec as P

H = 4
HD = 32
SEQ = 1024
NZ = 8
BLK = 64
HALF = SEQ // 2
NU = 3
NP = 2 * NU
NCHIP = 8
B = 256
NJ = HALF // B
R = 16
SUB = B // 2
LOG2E = 1.4426950408889634
SCALE = HD**-0.5
F32 = jnp.float32
BF16 = jnp.bfloat16
MESH = pl.DeviceIdType.MESH


def nn(a, b):
    return lax.dot_general(a, b, (((1,), (0,)), ((), ())), preferred_element_type=F32)


def wait_for(ref, sem):
    pltpu.make_async_copy(ref, ref, sem).wait()


def send(src, dst, send_sem, recv_sem, where):
    pltpu.make_async_remote_copy(
        src_ref=src,
        dst_ref=dst,
        send_sem=send_sem,
        recv_sem=recv_sem,
        device_id=where,
        device_id_type=MESH,
    ).start()


def at(index, size):
    return pl.ds(pl.multiple_of(index * size, size), size)


def kernel(
    len_ref, q_ref, k_ref, v_ref, g_ref, bias_ref,
    gq, gkv, fin,
    tsend, kv, qd, bias_full, b2, kvt, qdt, lhs, s_ref, dp_ref, ph, dsh, acc, dqt, g32,
    psend, precv, gqsend, gkvsend, db, sib, rsend, red, fsend,
    kv_ss, kv_rs, qd_ss, qd_rs, fw_ss, fw_rs, b1_ss, b1_rs, b1_ls, b2_ss, b2_rs, by_ss, by_rs, b3_ss, b3_rs,
    p_ss, p_rs, gq_ss, gq_rs, gk_ss, gk_rs, a_ss, a_rs, r_ss, r_rs, f_ss, f_rs,
):
    row = lax.axis_index("row")
    me = lax.axis_index("col")
    z = me % NZ
    yh = me // NZ
    chip = row // 2
    core = row % 2
    sibling = {"row": row + 1 - 2 * core}
    partner = {"col": (1 - yh) * NZ + z}
    others = [lax.rem(z + o, NZ) for o in range(1, NZ)]
    chips = [lax.rem(chip + o, NCHIP) for o in range(1, NCHIP)]

    def along_z(to):
        return {"col": yh * NZ + to}

    def along_row(to):
        return {"row": 2 * to + core}

    barrier = pltpu.get_barrier_semaphore()
    everyone = [along_z(to) for to in others] + [along_row(to) for to in chips] + [sibling, partner]
    everyone += [along_z(to) | sibling for to in others]
    for where in everyone:
        pl.semaphore_signal(barrier, inc=1, device_id=where, device_id_type=MESH)

    lane_block = lax.broadcasted_iota(jnp.int32, (BLK, 128), 1) // HD

    def lanes_from(parts):
        out = None
        for a, (x, b) in enumerate(parts):
            d = (a - b) % 4
            x = x if d == 0 else pltpu.roll(x, d * HD, 1)
            out = x if out is None else jnp.where(lane_block == a, x, out)
        return out

    def pack(u):
        for c in range(2):
            for kind, refs in enumerate(((k_ref, v_ref), (q_ref, g_ref))):
                arrays = [ref[c, 2 * u + e].astype(F32) for e in range(2) for ref in refs]
                for h in range(H):
                    tsend[u, kind, c * H + h] = lanes_from([(x, h) for x in arrays]).astype(BF16)
        kv[u, at(me, BLK), :] = tsend[u, 0, z]
        qd[u, at(z, BLK), :] = tsend[u, 1, z]

    def send_kv(u):
        for to in others:
            send(tsend.at[u, 0, to], kv.at[u, at(me, BLK)], kv_ss.at[u], kv_rs.at[u], along_z(to))

    def send_qd(u):
        for to in others:
            send(tsend.at[u, 1, to], qd.at[u, at(z, BLK)], qd_ss.at[u], qd_rs.at[u], along_z(to))

    def forward(u):
        wait_for(kv.at[u, pl.ds(0, BLK * (NZ - 1))], kv_rs.at[u])
        mine = kv.at[u, at(yh, HALF)]
        send(mine, mine, fw_ss.at[u], fw_rs.at[u], partner)

    ylo = chip // 4
    my_rows = pl.ds(pl.multiple_of(core * 32 + ylo * 16, 16), 16)
    their_rows = pl.ds(pl.multiple_of(core * 32 + (1 - ylo) * 16, 16), 16)
    my_lanes = at(chip % 4, 256)
    x_chips = [ylo * 4 + (chip + o) % 4 for o in range(1, 4)]
    y_chip = (1 - ylo) * 4 + chip % 4

    def bias_to_chips(jb):
        mine = bias_full.at[pl.ds(jb * 4, 4), my_rows, my_lanes]
        send(mine, mine, by_ss.at[jb], by_rs.at[jb], along_row(y_chip))
        for to in x_chips:
            send(mine, mine, b2_ss.at[jb], b2_rs.at[jb], along_row(to))

    def bias_onward(jb):
        theirs = bias_full.at[pl.ds(jb * 4, 4), their_rows, my_lanes]
        wait_for(theirs, by_rs.at[jb])
        for to in x_chips:
            send(theirs, theirs, b2_ss.at[jb], b2_rs.at[jb], along_row(to))

    def bias_to_sibling(jb):
        wait_for(bias_full.at[pl.ds(0, 6), :, pl.ds(0, 256)], b2_rs.at[jb])
        mine = bias_full.at[pl.ds(jb * 4, 4), at(core, 32)]
        send(mine, mine, b3_ss.at[jb], b3_rs.at[jb], sibling)

    pack(0)
    pack(1)
    pl.semaphore_wait(barrier, len(everyone))
    for to in others:
        send(
            bias_ref.at[to // H, to % H, my_rows, my_lanes],
            bias_full.at[z, my_rows, my_lanes],
            b1_ss,
            b1_rs,
            along_z(to),
        )
    own = pltpu.make_async_copy(
        bias_ref.at[z // H, z % H, my_rows, my_lanes], bias_full.at[z, my_rows, my_lanes], b1_ls
    )
    own.start()
    send_kv(0)
    send_qd(0)
    own.wait()
    wait_for(bias_full.at[pl.ds(0, NZ - 1), pl.ds(0, 16), pl.ds(0, 256)], b1_rs)
    bias_to_chips(0)
    bias_to_chips(1)
    send_kv(1)
    send_qd(1)
    pack(2)
    send_kv(2)
    send_qd(2)
    bias_onward(0)
    bias_onward(1)
    forward(0)
    bias_to_sibling(0)
    n = len_ref[z // H]
    db[...] = jnp.zeros_like(db)

    def mask_bias(jb):
        col = lax.broadcasted_iota(jnp.int32, (R, SEQ), 1)
        for c in range(B // R):
            x = bias_full[jb * 4 + c // 4, pl.ds((c % 4) * R, R), :].astype(F32)
            b2[pl.ds(pl.multiple_of(jb * B + c * R, R), R), :] = jnp.where(col < n, x * LOG2E, -1e30)

    def prep(u):
        wait_for(qd.at[u, pl.ds(0, BLK * (NZ - 1))], qd_rs.at[u])
        x = qd[u]
        qdt[...] = x.T
        block = lax.broadcasted_iota(jnp.int32, x.shape, 1) // HD
        for b in range(4):
            lhs[b] = jnp.where(block == b, x, jnp.zeros_like(x))
        wait_for(kv.at[u, pl.ds(0, HALF)], fw_rs.at[u])
        x = kv[u]
        kvt[...] = x.T
        acc[...] = jnp.zeros_like(acc)
        dqt[...] = jnp.zeros_like(dqt)

    def tile(jb):
        j0 = pl.multiple_of(jb * B, B)
        rows = pl.ds(j0, B)
        keys = kvt[...]
        for e in range(2):
            s_ref[e] = nn(lhs[2 * e, rows, :], keys)
            dp_ref[e] = nn(lhs[2 * e + 1, rows, :], keys)
        for c in range(B // R):
            r = pl.ds(c * R, R)
            jr = pl.ds(pl.multiple_of(j0 + c * R, R), R)
            total = db[jr, :]
            for e in range(2):
                s = s_ref[e, r, :] * (SCALE * LOG2E) + b2[jr, :]
                m = jnp.max(s, axis=1, keepdims=True)
                w = jnp.exp2(s - m)
                dp = dp_ref[e, r, :]
                rl = 1.0 / jnp.sum(w, axis=1, keepdims=True)
                delta = jnp.sum(w * dp, axis=1, keepdims=True) * rl
                pr = w * rl
                ds = pr * (dp - delta)
                ph[e, r, :] = pr.astype(BF16)
                dsh[e, r, :] = ds.astype(BF16)
                total = total + ds
            db[jr, :] = total
        for e in range(2):
            dsv = dsh[e]
            first, second = pl.ds(e * 64, HD), pl.ds(e * 64 + HD, HD)
            dqt[pl.ds(e * HD, HD), rows] += lax.dot_general(
                kvt[first, :], dsv, (((1,), (1,)), ((), ())), preferred_element_type=F32
            )
            acc[first, :] += nn(qdt[first, rows], dsv)
            acc[second, :] += nn(qdt[second, rows], ph[e])

    def finish_kv(u):
        even = (lax.broadcasted_iota(jnp.int32, (SEQ, 128), 1) // HD) % 2 == 0
        g = acc[...].T
        g = jnp.where(even, g * SCALE, g).reshape(2 * NZ, BLK, 128)
        top, low = g[:, :32], g[:, 32:]
        lane = lax.broadcasted_iota(jnp.int32, top.shape, 2)
        g32[0] = jnp.where(lane < 64, top, pltpu.roll(low, 64, 2))
        g32[1] = jnp.where(lane < 64, pltpu.roll(top, 64, 2), low)
        for e in range(2):
            p = 2 * u + e
            psend[p] = g32[e, at(1 - yh, NZ)].astype(BF16)
            send(psend.at[p], precv.at[p], p_ss.at[p], p_rs.at[p], partner)

    def finish_q(u):
        x = jnp.concatenate([dqt[...] * SCALE, jnp.zeros_like(dqt)], axis=0).T
        x = x.reshape(NZ, BLK, 128)
        lane = lax.broadcasted_iota(jnp.int32, (NZ, 32, 128), 2)
        gqsend[u] = jnp.where(lane < 64, x[:, :32], pltpu.roll(x[:, 32:], 64, 2)).astype(BF16)
        gq[u, z] = gqsend[u, z]
        for to in others:
            send(gqsend.at[u, to], gq.at[u, z], gq_ss.at[u], gq_rs.at[u], along_z(to))

    def combine(p):
        wait_for(precv.at[p], p_rs.at[p])
        gkvsend[p] = (g32[p % 2, at(yh, NZ)] + precv[p].astype(F32)).astype(BF16)
        gkv[p, z] = gkvsend[p, z]
        for to in others:
            send(gkvsend.at[p, to], gkv.at[p, z], gk_ss.at[p], gk_rs.at[p], along_z(to))

    def db_to_sibling(jb):
        theirs = db.at[pl.ds(pl.multiple_of(jb * B + (1 - core) * SUB, SUB), SUB)]
        send(theirs, sib.at[jb], a_ss.at[jb], a_rs.at[jb], sibling)

    def db_over_row(jb):
        wait_for(sib.at[jb], a_rs.at[jb])
        mine = pl.ds(pl.multiple_of(jb * B + core * SUB, SUB), SUB)
        for o in range(NCHIP):
            lanes = pl.ds(o * 128, 128)
            rsend[jb, o] = (db[mine, lanes] + sib[jb, :, lanes]).astype(BF16)
        red[jb, chip] = rsend[jb, chip]
        for to in chips:
            send(rsend.at[jb, to], red.at[jb, chip], r_ss.at[jb], r_rs.at[jb], along_row(to))

    def db_to_owner(jb):
        wait_for(red.at[jb, pl.ds(0, NCHIP - 1)], r_rs.at[jb])
        total = red[jb, 0].astype(F32)
        for o in range(1, NCHIP):
            total = total + red[jb, o].astype(F32)
        lane = lax.broadcasted_iota(jnp.int32, (32, 128), 1)
        for e in range(2):
            to = jb * 4 + core * 2 + e
            top = total[e * BLK : e * BLK + 32]
            low = total[e * BLK + 32 : (e + 1) * BLK]
            fsend[jb * 4 + e * 2] = jnp.where(lane < 64, top, pltpu.roll(low, 64, 1))
            fsend[jb * 4 + e * 2 + 1] = jnp.where(lane < 64, pltpu.roll(top, 64, 1), low)
            for a in range(2):
                mine = (to == z) & (core == a)

                @pl.when(mine)
                def _():
                    fin[z] = fsend[jb * 4 + e * 2 + a]

                @pl.when(jnp.logical_not(mine))
                def _():
                    where = along_z(to) | {"row": 2 * chip + a}
                    send(fsend.at[jb * 4 + e * 2 + a], fin.at[z], f_ss, f_rs, where)

    @pl.loop(0, NP)
    def _(it):
        u = it // NJ
        jb = it % NJ

        @pl.when(jb == 0)
        def _():
            prep(u)

        @pl.when(u == 0)
        def _():
            @pl.when(jb == 0)
            def _():
                bias_to_sibling(1)

            wait_for(bias_full.at[pl.ds(0, 4), pl.ds(0, 32)], b3_rs.at[jb])
            mask_bias(jb)

        @pl.when((jb == 0) & (u < NU - 1))
        def _():
            forward(u + 1)

        @pl.when((jb == 1) & (u > 0))
        def _():
            combine(2 * u - 2)

        tile(jb)

        @pl.when(u == NU - 1)
        def _():
            db_to_sibling(jb)

        @pl.when(it == NP - 1)
        def _():
            db_over_row(0)

        @pl.when((jb == 1) & (u > 0))
        def _():
            combine(2 * u - 1)

        @pl.when(jb == 1)
        def _():
            finish_kv(u)
            finish_q(u)

    db_over_row(1)
    combine(NP - 2)
    db_to_owner(0)
    combine(NP - 1)
    db_to_owner(1)
    owner = (z // 2) % 2 == core

    @pl.when(owner)
    def _():
        wait_for(fin.at[pl.ds(0, NZ - 1)], f_rs)
        wait_for(fsend.at[pl.ds(0, NZ - 1)], f_ss)

    @pl.when(jnp.logical_not(owner))
    def _():
        wait_for(fin, f_rs)
        wait_for(fsend, f_ss)

    wait_for(bias_full.at[pl.ds(0, NZ - 1), pl.ds(0, 16), pl.ds(0, 256)], b1_ss)
    for u in range(NU):
        wait_for(gq.at[u, pl.ds(0, NZ - 1)], gq_rs.at[u])
        wait_for(gq.at[u, pl.ds(0, NZ - 1)], gq_ss.at[u])
        wait_for(kv.at[u, pl.ds(0, BLK * (NZ - 1))], kv_ss.at[u])
        wait_for(qd.at[u, pl.ds(0, BLK * (NZ - 1))], qd_ss.at[u])
        wait_for(kv.at[u, pl.ds(0, HALF)], fw_ss.at[u])
    for p in range(NP):
        wait_for(gkv.at[p, pl.ds(0, NZ - 1)], gk_rs.at[p])
        wait_for(gkv.at[p, pl.ds(0, NZ - 1)], gk_ss.at[p])
        wait_for(psend.at[p], p_ss.at[p])
    for jb in range(NJ):
        wait_for(bias_full.at[pl.ds(0, 6), :, pl.ds(0, 256)], b2_ss.at[jb])
        wait_for(bias_full.at[pl.ds(0, 4), pl.ds(0, 16), pl.ds(0, 256)], by_ss.at[jb])
        wait_for(bias_full.at[pl.ds(0, 4), pl.ds(0, 32)], b3_ss.at[jb])
        wait_for(sib.at[jb], a_ss.at[jb])
        wait_for(red.at[jb, pl.ds(0, NCHIP - 1)], r_ss.at[jb])


def unpack(gq, gkv, fin, dq_out, dk_out, dv_out, db_out):
    lane_block = lax.broadcasted_iota(jnp.int32, (BLK, 128), 1) // HD

    def lanes_from(parts):
        out = None
        for h, (x, b) in enumerate(parts):
            d = (h - b) % 4
            x = x if d == 0 else pltpu.roll(x, d * HD, 1)
            out = x if out is None else jnp.where(lane_block == h, x, out)
        return out

    def unfold(parts, lanes):
        parts = [x.astype(F32) for x in parts]
        return [jnp.concatenate([x, pltpu.roll(x, 128 - lanes, 1)], axis=0) for x in parts]

    for u in range(NU):
        folded = unfold([gq[u, h] for h in range(H)], 64)
        for e in range(2):
            pairs = unfold([gkv[2 * u + e, h] for h in range(H)], 64)
            dq_out[0, 2 * u + e] = lanes_from([(x, e) for x in folded])
            dk_out[0, 2 * u + e] = lanes_from([(x, 0) for x in pairs])
            dv_out[0, 2 * u + e] = lanes_from([(x, 1) for x in pairs])
    for h in range(H):
        x = fin[h]
        db_out[0, h, :32] = x[:, :64]
        db_out[0, h, 32:] = pltpu.roll(x, 64, 1)[:, :64]


def per_device(query, key, value, grad_out, pair_bias, crop_lengths):
    V = pltpu.VMEM
    D = pltpu.SemaphoreType.DMA
    vm = pl.BlockSpec(memory_space=V)
    gq, gkv, fin = pl.pallas_call(
        kernel,
        out_shape=(
            jax.ShapeDtypeStruct((NU, NZ, 32, 128), BF16),
            jax.ShapeDtypeStruct((NP, NZ, 32, 128), BF16),
            jax.ShapeDtypeStruct((NZ, 32, 128), F32),
        ),
        in_specs=[pl.BlockSpec(memory_space=pltpu.SMEM)] + [vm] * 5,
        out_specs=(vm, vm, vm),
        scratch_shapes=[
            V((NU, 2, NZ, BLK, 128), BF16),
            V((NU, SEQ, 128), BF16),
            V((NU, HALF, 128), BF16),
            V((NZ, BLK, SEQ), BF16),
            V((HALF, SEQ), F32),
            V((128, SEQ), BF16),
            V((128, HALF), BF16),
            V((4, HALF, 128), BF16),
            V((2, B, SEQ), F32),
            V((2, B, SEQ), F32),
            V((2, B, SEQ), BF16),
            V((2, B, SEQ), BF16),
            V((128, SEQ), F32),
            V((64, HALF), F32),
            V((2, 2 * NZ, 32, 128), F32),
            V((NP, NZ, 32, 128), BF16),
            V((NP, NZ, 32, 128), BF16),
            V((NU, NZ, 32, 128), BF16),
            V((NP, NZ, 32, 128), BF16),
            V((HALF, SEQ), F32),
            V((NJ, SUB, SEQ), F32),
            V((NJ, NCHIP, SUB, 128), BF16),
            V((NJ, NCHIP, SUB, 128), BF16),
            V((NZ, 32, 128), F32),
        ]
        + [D((NU,))] * 6
        + [D] * 3
        + [D((NJ,))] * 6
        + [D((NP,))] * 2
        + [D((NU,))] * 2
        + [D((NP,))] * 2
        + [D((NJ,))] * 4
        + [D] * 2,
        compiler_params=pltpu.CompilerParams(
            vmem_limit_bytes=60 * 2**20, collective_id=0, has_side_effects=True
        ),
        cost_estimate=pl.CostEstimate(flops=8 * 10**9, bytes_accessed=4 * 10**6, transcendentals=3 * 2**20),
    )(crop_lengths, query, key, value, grad_out, pair_bias)
    grad = jax.ShapeDtypeStruct(query.shape, F32)
    spec = pl.BlockSpec((1, 6, BLK, 128), lambda c: (c, 0, 0, 0))
    return pl.pallas_call(
        unpack,
        grid=(2,),
        out_shape=(grad, grad, grad, jax.ShapeDtypeStruct((2, H, BLK, BLK), F32)),
        in_specs=[
            pl.BlockSpec((NU, H, 32, 128), lambda c: (0, c, 0, 0)),
            pl.BlockSpec((NP, H, 32, 128), lambda c: (0, c, 0, 0)),
            pl.BlockSpec((H, 32, 128), lambda c: (c, 0, 0)),
        ],
        out_specs=(spec, spec, spec, pl.BlockSpec((1, H, BLK, BLK), lambda c: (c, 0, 0, 0))),
    )(gq, gkv, fin)


def solution(mesh):
    spec = P(None, "row", "col", None)
    return jax.shard_map(
        per_device,
        mesh=mesh,
        in_specs=(spec, spec, spec, spec, P(None, None, "col", None), P()),
        out_specs=(spec, spec, spec, P(None, None, "col", "row")),
        check_vma=False,
    )
```

```python
import jax
import jax.numpy as jnp
from jax import lax
from jax.experimental import pallas as pl
from jax.experimental.pallas import tpu as pltpu
from jax.sharding import PartitionSpec as P

H = 4
HD = 32
SEQ = 1024
NZ = 8
BLK = 64
HALF = SEQ // 2
NU = 3
NP = 2 * NU
NCHIP = 8
B = 256
NJ = HALF // B
R = 16
SUB = B // 2
LOG2E = 1.4426950408889634
SCALE = HD**-0.5
F32 = jnp.float32
BF16 = jnp.bfloat16
MESH = pl.DeviceIdType.MESH


def nn(a, b):
    return lax.dot_general(a, b, (((1,), (0,)), ((), ())), preferred_element_type=F32)


def wait_for(ref, sem):
    pltpu.make_async_copy(ref, ref, sem).wait()


def send(src, dst, send_sem, recv_sem, where):
    pltpu.make_async_remote_copy(
        src_ref=src,
        dst_ref=dst,
        send_sem=send_sem,
        recv_sem=recv_sem,
        device_id=where,
        device_id_type=MESH,
    ).start()


def at(index, size):
    return pl.ds(pl.multiple_of(index * size, size), size)


def kernel(
    len_ref, q_hbm, k_hbm, v_hbm, g_hbm, bias_ref,
    gq, gkv, fin,
    q_ref, k_ref, v_ref, g_ref, tsend, kv, qd, bias_full, b2, kvt, qdt, s_ref, dp_ref, ph, dsh, acc, dqt, g32,
    psend, precv, gqsend, gkvsend, db, sib, rsend, red, redx, ysend, yrecv, fsend,
    kv_ss, kv_rs, qd_ss, qd_rs, fw_ss, fw_rs, b1_ss, b1_rs, b1_ls, b2_ss, b2_rs, by_ss, by_rs, b3_ss, b3_rs,
    p_ss, p_rs, gq_ss, gq_rs, gk_ss, gk_rs, a_ss, a_rs, r_ss, r_rs, f_ss, f_rs, y_ss, y_rs, in_ls,
):
    row = lax.axis_index("row")
    me = lax.axis_index("col")
    z = me % NZ
    yh = me // NZ
    chip = row // 2
    core = row % 2
    sibling = {"row": row + 1 - 2 * core}
    partner = {"col": (1 - yh) * NZ + z}
    others = [lax.rem(z + o, NZ) for o in range(1, NZ)]
    chips = [lax.rem(chip + o, NCHIP) for o in range(1, NCHIP)]

    def along_z(to):
        return {"col": yh * NZ + to}

    def along_row(to):
        return {"row": 2 * to + core}

    barrier = pltpu.get_barrier_semaphore()
    everyone = [along_z(to) for to in others] + [along_row(to) for to in chips] + [sibling, partner]
    everyone += [along_z(to) | sibling for to in others]
    for where in everyone:
        pl.semaphore_signal(barrier, inc=1, device_id=where, device_id_type=MESH)
    loads = [
        pltpu.make_async_copy(src, dst, in_ls.at[i])
        for i, (src, dst) in enumerate(((k_hbm, k_ref), (v_hbm, v_ref), (q_hbm, q_ref), (g_hbm, g_ref)))
    ]
    for load in loads:
        load.start()

    lane_block = lax.broadcasted_iota(jnp.int32, (BLK, 128), 1) // HD

    def lanes_from(parts):
        out = None
        for a, (x, b) in enumerate(parts):
            d = (a - b) % 4
            x = x if d == 0 else pltpu.roll(x, d * HD, 1)
            out = x if out is None else jnp.where(lane_block == a, x, out)
        return out

    def pack(u):
        for c in range(2):
            for kind, refs in enumerate(((k_ref, v_ref), (q_ref, g_ref))):
                arrays = [ref[c, 2 * u + e].astype(F32) for e in range(2) for ref in refs]
                for h in range(H):
                    tsend[u, kind, c * H + h] = lanes_from([(x, h) for x in arrays]).astype(BF16)
        kv[u, at(me, BLK), :] = tsend[u, 0, z]
        qd[u, at(z, BLK), :] = tsend[u, 1, z]

    def send_kv(u):
        for to in others:
            send(tsend.at[u, 0, to], kv.at[u, at(me, BLK)], kv_ss.at[u], kv_rs.at[u], along_z(to))

    def send_qd(u):
        for to in others:
            send(tsend.at[u, 1, to], qd.at[u, at(z, BLK)], qd_ss.at[u], qd_rs.at[u], along_z(to))

    def forward(u):
        wait_for(kv.at[u, pl.ds(0, BLK * (NZ - 1))], kv_rs.at[u])
        mine = kv.at[u, at(yh, HALF)]
        send(mine, mine, fw_ss.at[u], fw_rs.at[u], partner)

    ylo = chip // 4
    my_rows = pl.ds(pl.multiple_of(core * 32 + ylo * 16, 16), 16)
    their_rows = pl.ds(pl.multiple_of(core * 32 + (1 - ylo) * 16, 16), 16)
    my_lanes = at(chip % 4, 256)
    x_chips = [ylo * 4 + (chip + o) % 4 for o in range(1, 4)]
    y_chip = (1 - ylo) * 4 + chip % 4

    def bias_to_chips(jb):
        mine = bias_full.at[pl.ds(jb * 4, 4), my_rows, my_lanes]
        send(mine, mine, by_ss.at[jb], by_rs.at[jb], along_row(y_chip))
        for to in x_chips:
            send(mine, mine, b2_ss.at[jb], b2_rs.at[jb], along_row(to))

    def bias_onward(jb):
        theirs = bias_full.at[pl.ds(jb * 4, 4), their_rows, my_lanes]
        wait_for(theirs, by_rs.at[jb])
        for to in x_chips:
            send(theirs, theirs, b2_ss.at[jb], b2_rs.at[jb], along_row(to))

    def bias_to_sibling(jb):
        wait_for(bias_full.at[pl.ds(0, 6), :, pl.ds(0, 256)], b2_rs.at[jb])
        mine = bias_full.at[pl.ds(jb * 4, 4), at(core, 32)]
        send(mine, mine, b3_ss.at[jb], b3_rs.at[jb], sibling)

    for load in loads:
        load.wait()
    pack(0)
    pack(1)
    pl.semaphore_wait(barrier, len(everyone))
    for to in others:
        send(
            bias_ref.at[to // H, to % H, my_rows, my_lanes],
            bias_full.at[z, my_rows, my_lanes],
            b1_ss,
            b1_rs,
            along_z(to),
        )
    own = pltpu.make_async_copy(
        bias_ref.at[z // H, z % H, my_rows, my_lanes], bias_full.at[z, my_rows, my_lanes], b1_ls
    )
    own.start()
    send_kv(0)
    send_qd(0)
    own.wait()
    wait_for(bias_full.at[pl.ds(0, NZ - 1), pl.ds(0, 16), pl.ds(0, 256)], b1_rs)
    bias_to_chips(0)
    bias_to_chips(1)
    send_kv(1)
    pack(2)
    send_kv(2)
    send_qd(1)
    send_qd(2)
    bias_onward(0)
    bias_onward(1)
    forward(0)
    bias_to_sibling(0)
    n = len_ref[z // H]
    db[...] = jnp.zeros_like(db)

    def mask_bias(jb):
        col = lax.broadcasted_iota(jnp.int32, (R, SEQ), 1)
        for c in range(B // R):
            x = bias_full[jb * 4 + c // 4, pl.ds((c % 4) * R, R), :].astype(F32)
            b2[pl.ds(pl.multiple_of(jb * B + c * R, R), R), :] = jnp.where(col < n, x * LOG2E, -1e30)

    def prep(u):
        wait_for(qd.at[u, pl.ds(0, BLK * (NZ - 1))], qd_rs.at[u])
        x = qd[u]
        qdt[...] = x.T
        wait_for(kv.at[u, pl.ds(0, HALF)], fw_rs.at[u])
        x = kv[u]
        kvt[...] = x.T
        acc[...] = jnp.zeros_like(acc)
        dqt[...] = jnp.zeros_like(dqt)

    def tile(u, jb):
        j0 = pl.multiple_of(jb * B, B)
        rows = pl.ds(j0, B)
        for e in range(2):
            first, second = pl.ds(e * 64, HD), pl.ds(e * 64 + HD, HD)
            s_ref[e] = nn(qd[u, rows, first], kvt[first, :])
            dp_ref[e] = nn(qd[u, rows, second], kvt[second, :])
        for c in range(B // R):
            r = pl.ds(c * R, R)
            jr = pl.ds(pl.multiple_of(j0 + c * R, R), R)
            total = db[jr, :]
            for e in range(2):
                s = s_ref[e, r, :] * (SCALE * LOG2E) + b2[jr, :]
                m = jnp.max(s, axis=1, keepdims=True)
                w = jnp.exp2(s - m)
                dp = dp_ref[e, r, :]
                rl = 1.0 / jnp.sum(w, axis=1, keepdims=True)
                delta = jnp.sum(w * dp, axis=1, keepdims=True) * rl
                pr = w * rl
                ds = pr * (dp - delta)
                ph[e, r, :] = pr.astype(BF16)
                dsh[e, r, :] = ds.astype(BF16)
                total = total + ds
            db[jr, :] = total
        for e in range(2):
            dsv = dsh[e]
            first, second = pl.ds(e * 64, HD), pl.ds(e * 64 + HD, HD)
            dqt[pl.ds(e * HD, HD), rows] += lax.dot_general(
                kvt[first, :], dsv, (((1,), (1,)), ((), ())), preferred_element_type=F32
            )
            acc[first, :] += nn(qdt[first, rows], dsv)
            acc[second, :] += nn(qdt[second, rows], ph[e])

    def finish_kv(u):
        even = (lax.broadcasted_iota(jnp.int32, (SEQ, 128), 1) // HD) % 2 == 0
        g = acc[...].T
        g = jnp.where(even, g * SCALE, g).reshape(2 * NZ, BLK, 128)
        top, low = g[:, :32], g[:, 32:]
        lane = lax.broadcasted_iota(jnp.int32, top.shape, 2)
        g32[0] = jnp.where(lane < 64, top, pltpu.roll(low, 64, 2))
        g32[1] = jnp.where(lane < 64, pltpu.roll(top, 64, 2), low)
        for e in range(2):
            p = 2 * u + e
            psend[p] = g32[e, at(1 - yh, NZ)].astype(BF16)
            send(psend.at[p], precv.at[p], p_ss.at[p], p_rs.at[p], partner)

    def finish_q(u):
        x = jnp.concatenate([dqt[...] * SCALE, jnp.zeros_like(dqt)], axis=0).T
        x = x.reshape(NZ, BLK, 128)
        lane = lax.broadcasted_iota(jnp.int32, (NZ, 32, 128), 2)
        gqsend[u] = jnp.where(lane < 64, x[:, :32], pltpu.roll(x[:, 32:], 64, 2)).astype(BF16)
        gq[u, z] = gqsend[u, z]
        for to in others:
            send(gqsend.at[u, to], gq.at[u, z], gq_ss.at[u], gq_rs.at[u], along_z(to))

    def combine(p):
        wait_for(precv.at[p], p_rs.at[p])
        gkvsend[p] = (g32[p % 2, at(yh, NZ)] + precv[p].astype(F32)).astype(BF16)
        gkv[p, z] = gkvsend[p, z]
        for to in others:
            send(gkvsend.at[p, to], gkv.at[p, z], gk_ss.at[p], gk_rs.at[p], along_z(to))

    def db_to_sibling(jb):
        theirs = db.at[pl.ds(pl.multiple_of(jb * B + (1 - core) * SUB, SUB), SUB)]
        send(theirs, sib.at[jb], a_ss.at[jb], a_rs.at[jb], sibling)

    def db_over_row(jb):
        wait_for(sib.at[jb], a_rs.at[jb])
        mine = pl.ds(pl.multiple_of(jb * B + core * SUB, SUB), SUB)
        for o in range(NCHIP):
            lanes = pl.ds(o * 128, 128)
            rsend[jb, o] = (db[mine, lanes] + sib[jb, :, lanes]).astype(BF16)
        if jb == 0:
            redx[0, chip % 4] = rsend[0, chip]
            redx[1, chip % 4] = rsend[0, y_chip]
            for to in x_chips:
                send(rsend.at[0, to], redx.at[0, chip % 4], r_ss.at[0], r_rs.at[0], along_row(to))
                other = (1 - ylo) * 4 + to % 4
                send(rsend.at[0, other], redx.at[1, chip % 4], r_ss.at[0], r_rs.at[0], along_row(to))
        else:
            red[chip] = rsend[jb, chip]
            for to in chips:
                send(rsend.at[jb, to], red.at[chip], r_ss.at[jb], r_rs.at[jb], along_row(to))

    def db_cross():
        wait_for(rsend.at[0, pl.ds(0, 6)], r_rs.at[0])
        total = redx[1, 0].astype(F32)
        for o in range(1, 4):
            total = total + redx[1, o].astype(F32)
        ysend[...] = total
        send(ysend, yrecv, y_ss, y_rs, along_row(y_chip))

    def db_to_owner(jb):
        if jb == 0:
            wait_for(yrecv, y_rs)
            total = yrecv[...]
            for o in range(4):
                total = total + redx[0, o].astype(F32)
        else:
            wait_for(red.at[pl.ds(0, NCHIP - 1)], r_rs.at[jb])
            total = red[0].astype(F32)
            for o in range(1, NCHIP):
                total = total + red[o].astype(F32)
        lane = lax.broadcasted_iota(jnp.int32, (32, 128), 1)
        for e in range(2):
            to = jb * 4 + core * 2 + e
            top = total[e * BLK : e * BLK + 32]
            low = total[e * BLK + 32 : (e + 1) * BLK]
            fsend[jb * 4 + e * 2] = jnp.where(lane < 64, top, pltpu.roll(low, 64, 1))
            fsend[jb * 4 + e * 2 + 1] = jnp.where(lane < 64, pltpu.roll(top, 64, 1), low)
            for a in range(2):
                mine = (to == z) & (core == a)

                @pl.when(mine)
                def _():
                    fin[z] = fsend[jb * 4 + e * 2 + a]

                @pl.when(jnp.logical_not(mine))
                def _():
                    where = along_z(to) | {"row": 2 * chip + a}
                    send(fsend.at[jb * 4 + e * 2 + a], fin.at[z], f_ss, f_rs, where)

    @pl.loop(0, NP)
    def _(it):
        u = it // NJ
        jb = it % NJ

        @pl.when(jb == 0)
        def _():
            prep(u)

        @pl.when(u == 0)
        def _():
            @pl.when(jb == 0)
            def _():
                bias_to_sibling(1)

            wait_for(bias_full.at[pl.ds(0, 4), pl.ds(0, 32)], b3_rs.at[jb])
            mask_bias(jb)

        @pl.when(it < NU - 1)
        def _():
            forward(it + 1)

        tile(u, jb)

        @pl.when(u == NU - 1)
        def _():
            db_to_sibling(jb)

        @pl.when(it == NP - 1)
        def _():
            db_over_row(0)

        @pl.when((jb == 1) & (u > 0))
        def _():
            combine(2 * u - 2)
            combine(2 * u - 1)

        @pl.when(jb == 1)
        def _():
            finish_kv(u)
            finish_q(u)

    db_over_row(1)
    db_cross()
    combine(NP - 2)
    combine(NP - 1)
    db_to_owner(0)
    db_to_owner(1)
    wait_for(ysend, y_ss)
    owner = (z // 2) % 2 == core

    @pl.when(owner)
    def _():
        wait_for(fin.at[pl.ds(0, NZ - 1)], f_rs)
        wait_for(fsend.at[pl.ds(0, NZ - 1)], f_ss)

    @pl.when(jnp.logical_not(owner))
    def _():
        wait_for(fin, f_rs)
        wait_for(fsend, f_ss)

    wait_for(bias_full.at[pl.ds(0, NZ - 1), pl.ds(0, 16), pl.ds(0, 256)], b1_ss)
    for u in range(NU):
        wait_for(gq.at[u, pl.ds(0, NZ - 1)], gq_rs.at[u])
        wait_for(gq.at[u, pl.ds(0, NZ - 1)], gq_ss.at[u])
        wait_for(kv.at[u, pl.ds(0, BLK * (NZ - 1))], kv_ss.at[u])
        wait_for(qd.at[u, pl.ds(0, BLK * (NZ - 1))], qd_ss.at[u])
        wait_for(kv.at[u, pl.ds(0, HALF)], fw_ss.at[u])
    for p in range(NP):
        wait_for(gkv.at[p, pl.ds(0, NZ - 1)], gk_rs.at[p])
        wait_for(gkv.at[p, pl.ds(0, NZ - 1)], gk_ss.at[p])
        wait_for(psend.at[p], p_ss.at[p])
    for jb in range(NJ):
        wait_for(bias_full.at[pl.ds(0, 6), :, pl.ds(0, 256)], b2_ss.at[jb])
        wait_for(bias_full.at[pl.ds(0, 4), pl.ds(0, 16), pl.ds(0, 256)], by_ss.at[jb])
        wait_for(bias_full.at[pl.ds(0, 4), pl.ds(0, 32)], b3_ss.at[jb])
        wait_for(sib.at[jb], a_ss.at[jb])
        wait_for(rsend.at[jb, pl.ds(0, NCHIP - 1 if jb else 6)], r_ss.at[jb])


def unpack(gq, gkv, fin, dq_out, dk_out, dv_out, db_out):
    lane_block = lax.broadcasted_iota(jnp.int32, (BLK, 128), 1) // HD

    def lanes_from(parts):
        out = None
        for h, (x, b) in enumerate(parts):
            d = (h - b) % 4
            x = x if d == 0 else pltpu.roll(x, d * HD, 1)
            out = x if out is None else jnp.where(lane_block == h, x, out)
        return out

    def unfold(parts, lanes):
        parts = [x.astype(F32) for x in parts]
        return [jnp.concatenate([x, pltpu.roll(x, 128 - lanes, 1)], axis=0) for x in parts]

    for u in range(NU):
        folded = unfold([gq[u, h] for h in range(H)], 64)
        for e in range(2):
            pairs = unfold([gkv[2 * u + e, h] for h in range(H)], 64)
            dq_out[0, 2 * u + e] = lanes_from([(x, e) for x in folded])
            dk_out[0, 2 * u + e] = lanes_from([(x, 0) for x in pairs])
            dv_out[0, 2 * u + e] = lanes_from([(x, 1) for x in pairs])
    for h in range(H):
        x = fin[h]
        db_out[0, h, :32] = x[:, :64]
        db_out[0, h, 32:] = pltpu.roll(x, 64, 1)[:, :64]


def per_device(query, key, value, grad_out, pair_bias, crop_lengths):
    V = pltpu.VMEM
    D = pltpu.SemaphoreType.DMA
    vm = pl.BlockSpec(memory_space=V)
    gq, gkv, fin = pl.pallas_call(
        kernel,
        out_shape=(
            jax.ShapeDtypeStruct((NU, NZ, 32, 128), BF16),
            jax.ShapeDtypeStruct((NP, NZ, 32, 128), BF16),
            jax.ShapeDtypeStruct((NZ, 32, 128), F32),
        ),
        in_specs=[pl.BlockSpec(memory_space=pltpu.SMEM)] + [pl.BlockSpec(memory_space=pl.ANY)] * 5,
        out_specs=(vm, vm, vm),
        scratch_shapes=[V(query.shape, BF16)] * 4
        + [
            V((NU, 2, NZ, BLK, 128), BF16),
            V((NU, SEQ, 128), BF16),
            V((NU, HALF, 128), BF16),
            V((NZ, BLK, SEQ), BF16),
            V((HALF, SEQ), F32),
            V((128, SEQ), BF16),
            V((128, HALF), BF16),
            V((2, B, SEQ), F32),
            V((2, B, SEQ), F32),
            V((2, B, SEQ), BF16),
            V((2, B, SEQ), BF16),
            V((128, SEQ), F32),
            V((64, HALF), F32),
            V((2, 2 * NZ, 32, 128), F32),
            V((NP, NZ, 32, 128), BF16),
            V((NP, NZ, 32, 128), BF16),
            V((NU, NZ, 32, 128), BF16),
            V((NP, NZ, 32, 128), BF16),
            V((HALF, SEQ), F32),
            V((NJ, SUB, SEQ), F32),
            V((NJ, NCHIP, SUB, 128), BF16),
            V((NCHIP, SUB, 128), BF16),
            V((2, 4, SUB, 128), BF16),
            V((SUB, 128), F32),
            V((SUB, 128), F32),
            V((NZ, 32, 128), F32),
        ]
        + [D((NU,))] * 6
        + [D] * 3
        + [D((NJ,))] * 6
        + [D((NP,))] * 2
        + [D((NU,))] * 2
        + [D((NP,))] * 2
        + [D((NJ,))] * 4
        + [D] * 4
        + [D((4,))],
        compiler_params=pltpu.CompilerParams(
            vmem_limit_bytes=60 * 2**20, collective_id=0, has_side_effects=True
        ),
        cost_estimate=pl.CostEstimate(flops=8 * 10**9, bytes_accessed=4 * 10**6, transcendentals=3 * 2**20),
    )(crop_lengths, query, key, value, grad_out, pair_bias)
    grad = jax.ShapeDtypeStruct(query.shape, F32)
    spec = pl.BlockSpec((1, 6, BLK, 128), lambda c: (c, 0, 0, 0))
    return pl.pallas_call(
        unpack,
        grid=(2,),
        out_shape=(grad, grad, grad, jax.ShapeDtypeStruct((2, H, BLK, BLK), F32)),
        in_specs=[
            pl.BlockSpec((NU, H, 32, 128), lambda c: (0, c, 0, 0)),
            pl.BlockSpec((NP, H, 32, 128), lambda c: (0, c, 0, 0)),
            pl.BlockSpec((H, 32, 128), lambda c: (c, 0, 0)),
        ],
        out_specs=(spec, spec, spec, pl.BlockSpec((1, H, BLK, BLK), lambda c: (c, 0, 0, 0))),
    )(gq, gkv, fin)


def solution(mesh):
    spec = P(None, "row", "col", None)
    return jax.shard_map(
        per_device,
        mesh=mesh,
        in_specs=(spec, spec, spec, spec, P(None, None, "col", None), P()),
        out_specs=(spec, spec, spec, P(None, None, "col", "row")),
        check_vma=False,
    )
```

```python
import jax
import jax.numpy as jnp
from jax import lax
from jax.experimental import pallas as pl
from jax.experimental.pallas import tpu as pltpu
from jax.sharding import PartitionSpec as P

H = 4
HD = 32
SEQ = 1024
NZ = 8
BLK = 64
HALF = SEQ // 2
NU = 3
NP = 2 * NU
NCHIP = 8
B = 256
NJ = HALF // B
R = 16
SUB = B // 2
LOG2E = 1.4426950408889634
SCALE = HD**-0.5
F32 = jnp.float32
BF16 = jnp.bfloat16
MESH = pl.DeviceIdType.MESH


def nn(a, b):
    return lax.dot_general(a, b, (((1,), (0,)), ((), ())), preferred_element_type=F32)


def wait_for(ref, sem):
    pltpu.make_async_copy(ref, ref, sem).wait()


def send(src, dst, send_sem, recv_sem, where):
    pltpu.make_async_remote_copy(
        src_ref=src,
        dst_ref=dst,
        send_sem=send_sem,
        recv_sem=recv_sem,
        device_id=where,
        device_id_type=MESH,
    ).start()


def at(index, size):
    return pl.ds(pl.multiple_of(index * size, size), size)


def kernel(
    len_ref, q_hbm, k_hbm, v_hbm, g_hbm, bias_ref,
    gq, gkv, fin,
    q_ref, k_ref, v_ref, g_ref, tsend, kv, qd, bias_full, b2, kvt, qdt, s_ref, dp_ref, ph, dsh, acc, dqt, g32,
    psend, precv, gqsend, gkvsend, db, sib, rsend, red, redx, ysend, yrecv, fsend,
    kv_ss, kv_rs, qd_ss, qd_rs, fw_ss, fw_rs, b1_ss, b1_rs, b1_ls, b2_ss, b2_rs, by_ss, by_rs, b3_ss, b3_rs,
    p_ss, p_rs, gq_ss, gq_rs, gk_ss, gk_rs, a_ss, a_rs, r_ss, r_rs, f_ss, f_rs, y_ss, y_rs, in_ls,
):
    row = lax.axis_index("row")
    me = lax.axis_index("col")
    z = me % NZ
    yh = me // NZ
    chip = row // 2
    core = row % 2
    sibling = {"row": row + 1 - 2 * core}
    partner = {"col": (1 - yh) * NZ + z}
    others = [lax.rem(z + o, NZ) for o in range(1, NZ)]
    chips = [lax.rem(chip + o, NCHIP) for o in range(1, NCHIP)]

    def along_z(to):
        return {"col": yh * NZ + to}

    def along_row(to):
        return {"row": 2 * to + core}

    barrier = pltpu.get_barrier_semaphore()
    everyone = [along_z(to) for to in others] + [along_row(to) for to in chips] + [sibling, partner]
    everyone += [along_z(to) | sibling for to in others]
    for where in everyone:
        pl.semaphore_signal(barrier, inc=1, device_id=where, device_id_type=MESH)
    loads = [
        pltpu.make_async_copy(src, dst, in_ls.at[i])
        for i, (src, dst) in enumerate(((k_hbm, k_ref), (v_hbm, v_ref), (q_hbm, q_ref), (g_hbm, g_ref)))
    ]
    for load in loads:
        load.start()

    lane_block = lax.broadcasted_iota(jnp.int32, (BLK, 128), 1) // HD

    def lanes_from(parts):
        out = None
        for a, (x, b) in enumerate(parts):
            d = (a - b) % 4
            x = x if d == 0 else pltpu.roll(x, d * HD, 1)
            out = x if out is None else jnp.where(lane_block == a, x, out)
        return out

    def pack(u):
        for c in range(2):
            for kind, refs in enumerate(((k_ref, v_ref), (q_ref, g_ref))):
                arrays = [ref[c, 2 * u + e].astype(F32) for e in range(2) for ref in refs]
                for h in range(H):
                    tsend[u, kind, c * H + h] = lanes_from([(x, h) for x in arrays]).astype(BF16)
        kv[u, at(me, BLK), :] = tsend[u, 0, z]
        qd[u, at(z, BLK), :] = tsend[u, 1, z]

    def send_kv(u):
        for to in others:
            send(tsend.at[u, 0, to], kv.at[u, at(me, BLK)], kv_ss.at[u], kv_rs.at[u], along_z(to))

    def send_qd(u):
        for to in others:
            send(tsend.at[u, 1, to], qd.at[u, at(z, BLK)], qd_ss.at[u], qd_rs.at[u], along_z(to))

    def forward(u):
        wait_for(kv.at[u, pl.ds(0, BLK * (NZ - 1))], kv_rs.at[u])
        mine = kv.at[u, at(yh, HALF)]
        send(mine, mine, fw_ss.at[u], fw_rs.at[u], partner)

    ylo = chip // 4
    my_rows = pl.ds(pl.multiple_of(core * 32 + ylo * 16, 16), 16)
    their_rows = pl.ds(pl.multiple_of(core * 32 + (1 - ylo) * 16, 16), 16)
    my_lanes = at(chip % 4, 256)
    x_chips = [ylo * 4 + (chip + o) % 4 for o in range(1, 4)]
    y_chip = (1 - ylo) * 4 + chip % 4

    def bias_to_chips(jb):
        mine = bias_full.at[pl.ds(jb * 4, 4), my_rows, my_lanes]
        if jb == 1:
            send(mine, mine, by_ss.at[jb], by_rs.at[jb], along_row(y_chip))
        for to in x_chips if jb == 1 else chips:
            send(mine, mine, b2_ss.at[jb], b2_rs.at[jb], along_row(to))

    def bias_onward(jb):
        theirs = bias_full.at[pl.ds(jb * 4, 4), their_rows, my_lanes]
        wait_for(theirs, by_rs.at[jb])
        for to in x_chips:
            send(theirs, theirs, b2_ss.at[jb], b2_rs.at[jb], along_row(to))

    def bias_to_sibling(jb):
        wait_for(bias_full.at[pl.ds(0, 6 if jb else 7), :, pl.ds(0, 256)], b2_rs.at[jb])
        mine = bias_full.at[pl.ds(jb * 4, 4), at(core, 32)]
        send(mine, mine, b3_ss.at[jb], b3_rs.at[jb], sibling)

    for load in loads:
        load.wait()
    pack(0)
    pl.semaphore_wait(barrier, len(everyone))
    for to in others:
        send(
            bias_ref.at[to // H, to % H, my_rows, my_lanes],
            bias_full.at[z, my_rows, my_lanes],
            b1_ss,
            b1_rs,
            along_z(to),
        )
    own = pltpu.make_async_copy(
        bias_ref.at[z // H, z % H, my_rows, my_lanes], bias_full.at[z, my_rows, my_lanes], b1_ls
    )
    own.start()
    send_kv(0)
    send_qd(0)
    pack(1)
    own.wait()
    wait_for(bias_full.at[pl.ds(0, NZ - 1), pl.ds(0, 16), pl.ds(0, 256)], b1_rs)
    bias_to_chips(0)
    bias_to_chips(1)
    send_kv(1)
    pack(2)
    send_kv(2)
    send_qd(1)
    send_qd(2)
    bias_onward(1)
    forward(0)
    bias_to_sibling(0)
    n = len_ref[z // H]
    db[...] = jnp.zeros_like(db)

    def mask_bias(jb):
        col = lax.broadcasted_iota(jnp.int32, (R, SEQ), 1)
        for c in range(B // R):
            x = bias_full[jb * 4 + c // 4, pl.ds((c % 4) * R, R), :].astype(F32)
            b2[pl.ds(pl.multiple_of(jb * B + c * R, R), R), :] = jnp.where(col < n, x * LOG2E, -1e30)

    def prep(u):
        wait_for(qd.at[u, pl.ds(0, BLK * (NZ - 1))], qd_rs.at[u])
        x = qd[u]
        qdt[...] = x.T
        wait_for(kv.at[u, pl.ds(0, HALF)], fw_rs.at[u])
        x = kv[u]
        kvt[...] = x.T
        acc[...] = jnp.zeros_like(acc)
        dqt[...] = jnp.zeros_like(dqt)

    def tile(u, jb):
        j0 = pl.multiple_of(jb * B, B)
        rows = pl.ds(j0, B)
        for e in range(2):
            first, second = pl.ds(e * 64, HD), pl.ds(e * 64 + HD, HD)
            s_ref[e] = nn(qd[u, rows, first], kvt[first, :])
            dp_ref[e] = nn(qd[u, rows, second], kvt[second, :])
        for c in range(B // R):
            r = pl.ds(c * R, R)
            jr = pl.ds(pl.multiple_of(j0 + c * R, R), R)
            total = db[jr, :]
            for e in range(2):
                s = s_ref[e, r, :] * (SCALE * LOG2E) + b2[jr, :]
                m = jnp.max(s, axis=1, keepdims=True)
                w = jnp.exp2(s - m)
                dp = dp_ref[e, r, :]
                rl = 1.0 / jnp.sum(w, axis=1, keepdims=True)
                delta = jnp.sum(w * dp, axis=1, keepdims=True) * rl
                pr = w * rl
                ds = pr * (dp - delta)
                ph[e, r, :] = pr.astype(BF16)
                dsh[e, r, :] = ds.astype(BF16)
                total = total + ds
            db[jr, :] = total
        for e in range(2):
            dsv = dsh[e]
            first, second = pl.ds(e * 64, HD), pl.ds(e * 64 + HD, HD)
            dqt[pl.ds(e * HD, HD), rows] += lax.dot_general(
                kvt[first, :], dsv, (((1,), (1,)), ((), ())), preferred_element_type=F32
            )
            acc[first, :] += nn(qdt[first, rows], dsv)
            acc[second, :] += nn(qdt[second, rows], ph[e])

    def finish_kv(u):
        even = (lax.broadcasted_iota(jnp.int32, (SEQ, 128), 1) // HD) % 2 == 0
        g = acc[...].T
        g = jnp.where(even, g * SCALE, g).reshape(2 * NZ, BLK, 128)
        top, low = g[:, :32], g[:, 32:]
        lane = lax.broadcasted_iota(jnp.int32, top.shape, 2)
        g32[0] = jnp.where(lane < 64, top, pltpu.roll(low, 64, 2))
        g32[1] = jnp.where(lane < 64, pltpu.roll(top, 64, 2), low)
        for e in range(2):
            p = 2 * u + e
            psend[p] = g32[e, at(1 - yh, NZ)].astype(BF16)
            send(psend.at[p], precv.at[p], p_ss.at[p], p_rs.at[p], partner)

    def finish_q(u):
        x = jnp.concatenate([dqt[...] * SCALE, jnp.zeros_like(dqt)], axis=0).T
        x = x.reshape(NZ, BLK, 128)
        lane = lax.broadcasted_iota(jnp.int32, (NZ, 32, 128), 2)
        gqsend[u] = jnp.where(lane < 64, x[:, :32], pltpu.roll(x[:, 32:], 64, 2)).astype(BF16)
        gq[u, z] = gqsend[u, z]
        for to in others:
            send(gqsend.at[u, to], gq.at[u, z], gq_ss.at[u], gq_rs.at[u], along_z(to))

    def combine(p):
        wait_for(precv.at[p], p_rs.at[p])
        gkvsend[p] = (g32[p % 2, at(yh, NZ)] + precv[p].astype(F32)).astype(BF16)
        gkv[p, z] = gkvsend[p, z]
        for to in others:
            send(gkvsend.at[p, to], gkv.at[p, z], gk_ss.at[p], gk_rs.at[p], along_z(to))

    def db_to_sibling(jb):
        theirs = db.at[pl.ds(pl.multiple_of(jb * B + (1 - core) * SUB, SUB), SUB)]
        send(theirs, sib.at[jb], a_ss.at[jb], a_rs.at[jb], sibling)

    def db_over_row(jb):
        wait_for(sib.at[jb], a_rs.at[jb])
        mine = pl.ds(pl.multiple_of(jb * B + core * SUB, SUB), SUB)
        for o in range(NCHIP):
            lanes = pl.ds(o * 128, 128)
            rsend[jb, o] = (db[mine, lanes] + sib[jb, :, lanes]).astype(BF16)
        if jb == 0:
            redx[0, chip % 4] = rsend[0, chip]
            redx[1, chip % 4] = rsend[0, y_chip]
            for to in x_chips:
                send(rsend.at[0, to], redx.at[0, chip % 4], r_ss.at[0], r_rs.at[0], along_row(to))
                other = (1 - ylo) * 4 + to % 4
                send(rsend.at[0, other], redx.at[1, chip % 4], r_ss.at[0], r_rs.at[0], along_row(to))
        else:
            red[chip] = rsend[jb, chip]
            for to in chips:
                send(rsend.at[jb, to], red.at[chip], r_ss.at[jb], r_rs.at[jb], along_row(to))

    def db_cross():
        wait_for(rsend.at[0, pl.ds(0, 6)], r_rs.at[0])
        total = redx[1, 0].astype(F32)
        for o in range(1, 4):
            total = total + redx[1, o].astype(F32)
        ysend[...] = total
        send(ysend, yrecv, y_ss, y_rs, along_row(y_chip))

    def db_to_owner(jb):
        if jb == 0:
            wait_for(yrecv, y_rs)
            total = yrecv[...]
            for o in range(4):
                total = total + redx[0, o].astype(F32)
        else:
            wait_for(red.at[pl.ds(0, NCHIP - 1)], r_rs.at[jb])
            total = red[0].astype(F32)
            for o in range(1, NCHIP):
                total = total + red[o].astype(F32)
        lane = lax.broadcasted_iota(jnp.int32, (32, 128), 1)
        for e in range(2):
            to = jb * 4 + core * 2 + e
            top = total[e * BLK : e * BLK + 32]
            low = total[e * BLK + 32 : (e + 1) * BLK]
            fsend[jb * 4 + e * 2] = jnp.where(lane < 64, top, pltpu.roll(low, 64, 1))
            fsend[jb * 4 + e * 2 + 1] = jnp.where(lane < 64, pltpu.roll(top, 64, 1), low)
            for a in range(2):
                mine = (to == z) & (core == a)

                @pl.when(mine)
                def _():
                    fin[z] = fsend[jb * 4 + e * 2 + a]

                @pl.when(jnp.logical_not(mine))
                def _():
                    where = along_z(to) | {"row": 2 * chip + a}
                    send(fsend.at[jb * 4 + e * 2 + a], fin.at[z], f_ss, f_rs, where)

    @pl.loop(0, NP)
    def _(it):
        u = it // NJ
        jb = it % NJ

        @pl.when(jb == 0)
        def _():
            prep(u)

        @pl.when(u == 0)
        def _():
            @pl.when(jb == 0)
            def _():
                bias_to_sibling(1)

            wait_for(bias_full.at[pl.ds(0, 4), pl.ds(0, 32)], b3_rs.at[jb])
            mask_bias(jb)

        @pl.when(it < NU - 1)
        def _():
            forward(it + 1)

        tile(u, jb)

        @pl.when(u == NU - 1)
        def _():
            db_to_sibling(jb)

        @pl.when(it == NP - 1)
        def _():
            db_over_row(0)

        @pl.when((jb == 1) & (u > 0))
        def _():
            combine(2 * u - 2)
            combine(2 * u - 1)

        @pl.when(jb == 1)
        def _():
            finish_kv(u)
            finish_q(u)

    db_over_row(1)
    db_cross()
    combine(NP - 2)
    combine(NP - 1)
    db_to_owner(0)
    db_to_owner(1)
    wait_for(ysend, y_ss)
    owner = (z // 2) % 2 == core

    @pl.when(owner)
    def _():
        wait_for(fin.at[pl.ds(0, NZ - 1)], f_rs)
        wait_for(fsend.at[pl.ds(0, NZ - 1)], f_ss)

    @pl.when(jnp.logical_not(owner))
    def _():
        wait_for(fin, f_rs)
        wait_for(fsend, f_ss)

    wait_for(bias_full.at[pl.ds(0, NZ - 1), pl.ds(0, 16), pl.ds(0, 256)], b1_ss)
    for u in range(NU):
        wait_for(gq.at[u, pl.ds(0, NZ - 1)], gq_rs.at[u])
        wait_for(gq.at[u, pl.ds(0, NZ - 1)], gq_ss.at[u])
        wait_for(kv.at[u, pl.ds(0, BLK * (NZ - 1))], kv_ss.at[u])
        wait_for(qd.at[u, pl.ds(0, BLK * (NZ - 1))], qd_ss.at[u])
        wait_for(kv.at[u, pl.ds(0, HALF)], fw_ss.at[u])
    for p in range(NP):
        wait_for(gkv.at[p, pl.ds(0, NZ - 1)], gk_rs.at[p])
        wait_for(gkv.at[p, pl.ds(0, NZ - 1)], gk_ss.at[p])
        wait_for(psend.at[p], p_ss.at[p])
    for jb in range(NJ):
        wait_for(bias_full.at[pl.ds(0, 6 if jb else 7), :, pl.ds(0, 256)], b2_ss.at[jb])
        if jb == 1:
            wait_for(bias_full.at[pl.ds(0, 4), pl.ds(0, 16), pl.ds(0, 256)], by_ss.at[jb])
        wait_for(bias_full.at[pl.ds(0, 4), pl.ds(0, 32)], b3_ss.at[jb])
        wait_for(sib.at[jb], a_ss.at[jb])
        wait_for(rsend.at[jb, pl.ds(0, NCHIP - 1 if jb else 6)], r_ss.at[jb])


def unpack(gq, gkv, fin, dq_out, dk_out, dv_out, db_out):
    lane_block = lax.broadcasted_iota(jnp.int32, (BLK, 128), 1) // HD

    def lanes_from(parts):
        out = None
        for h, (x, b) in enumerate(parts):
            d = (h - b) % 4
            x = x if d == 0 else pltpu.roll(x, d * HD, 1)
            out = x if out is None else jnp.where(lane_block == h, x, out)
        return out

    def unfold(parts, lanes):
        parts = [x.astype(F32) for x in parts]
        return [jnp.concatenate([x, pltpu.roll(x, 128 - lanes, 1)], axis=0) for x in parts]

    for u in range(NU):
        folded = unfold([gq[u, h] for h in range(H)], 64)
        for e in range(2):
            pairs = unfold([gkv[2 * u + e, h] for h in range(H)], 64)
            dq_out[0, 2 * u + e] = lanes_from([(x, e) for x in folded])
            dk_out[0, 2 * u + e] = lanes_from([(x, 0) for x in pairs])
            dv_out[0, 2 * u + e] = lanes_from([(x, 1) for x in pairs])
    for h in range(H):
        x = fin[h]
        db_out[0, h, :32] = x[:, :64]
        db_out[0, h, 32:] = pltpu.roll(x, 64, 1)[:, :64]


def per_device(query, key, value, grad_out, pair_bias, crop_lengths):
    V = pltpu.VMEM
    D = pltpu.SemaphoreType.DMA
    vm = pl.BlockSpec(memory_space=V)
    gq, gkv, fin = pl.pallas_call(
        kernel,
        out_shape=(
            jax.ShapeDtypeStruct((NU, NZ, 32, 128), BF16),
            jax.ShapeDtypeStruct((NP, NZ, 32, 128), BF16),
            jax.ShapeDtypeStruct((NZ, 32, 128), F32),
        ),
        in_specs=[pl.BlockSpec(memory_space=pltpu.SMEM)] + [pl.BlockSpec(memory_space=pl.ANY)] * 5,
        out_specs=(vm, vm, vm),
        scratch_shapes=[V(query.shape, BF16)] * 4
        + [
            V((NU, 2, NZ, BLK, 128), BF16),
            V((NU, SEQ, 128), BF16),
            V((NU, HALF, 128), BF16),
            V((NZ, BLK, SEQ), BF16),
            V((HALF, SEQ), F32),
            V((128, SEQ), BF16),
            V((128, HALF), BF16),
            V((2, B, SEQ), F32),
            V((2, B, SEQ), F32),
            V((2, B, SEQ), BF16),
            V((2, B, SEQ), BF16),
            V((128, SEQ), F32),
            V((64, HALF), F32),
            V((2, 2 * NZ, 32, 128), F32),
            V((NP, NZ, 32, 128), BF16),
            V((NP, NZ, 32, 128), BF16),
            V((NU, NZ, 32, 128), BF16),
            V((NP, NZ, 32, 128), BF16),
            V((HALF, SEQ), F32),
            V((NJ, SUB, SEQ), F32),
            V((NJ, NCHIP, SUB, 128), BF16),
            V((NCHIP, SUB, 128), BF16),
            V((2, 4, SUB, 128), BF16),
            V((SUB, 128), F32),
            V((SUB, 128), F32),
            V((NZ, 32, 128), F32),
        ]
        + [D((NU,))] * 6
        + [D] * 3
        + [D((NJ,))] * 6
        + [D((NP,))] * 2
        + [D((NU,))] * 2
        + [D((NP,))] * 2
        + [D((NJ,))] * 4
        + [D] * 4
        + [D((4,))],
        compiler_params=pltpu.CompilerParams(
            vmem_limit_bytes=60 * 2**20, collective_id=0, has_side_effects=True
        ),
        cost_estimate=pl.CostEstimate(flops=8 * 10**9, bytes_accessed=4 * 10**6, transcendentals=3 * 2**20),
    )(crop_lengths, query, key, value, grad_out, pair_bias)
    grad = jax.ShapeDtypeStruct(query.shape, F32)
    spec = pl.BlockSpec((1, 6, BLK, 128), lambda c: (c, 0, 0, 0))
    return pl.pallas_call(
        unpack,
        grid=(2,),
        out_shape=(grad, grad, grad, jax.ShapeDtypeStruct((2, H, BLK, BLK), F32)),
        in_specs=[
            pl.BlockSpec((NU, H, 32, 128), lambda c: (0, c, 0, 0)),
            pl.BlockSpec((NP, H, 32, 128), lambda c: (0, c, 0, 0)),
            pl.BlockSpec((H, 32, 128), lambda c: (c, 0, 0)),
        ],
        out_specs=(spec, spec, spec, pl.BlockSpec((1, H, BLK, BLK), lambda c: (c, 0, 0, 0))),
    )(gq, gkv, fin)


def solution(mesh):
    spec = P(None, "row", "col", None)
    return jax.shard_map(
        per_device,
        mesh=mesh,
        in_specs=(spec, spec, spec, spec, P(None, None, "col", None), P()),
        out_specs=(spec, spec, spec, P(None, None, "col", "row")),
        check_vma=False,
    )
```

```python
import jax
import jax.numpy as jnp
from jax import lax
from jax.experimental import pallas as pl
from jax.experimental.pallas import tpu as pltpu
from jax.sharding import PartitionSpec as P

H = 4
HD = 32
SEQ = 1024
NZ = 8
BLK = 64
HALF = SEQ // 2
NU = 3
NP = 2 * NU
NCHIP = 8
B = 256
NJ = HALF // B
R = 16
SUB = B // 2
LOG2E = 1.4426950408889634
SCALE = HD**-0.5
F32 = jnp.float32
BF16 = jnp.bfloat16
MESH = pl.DeviceIdType.MESH


def nn(a, b):
    return lax.dot_general(a, b, (((1,), (0,)), ((), ())), preferred_element_type=F32)


def wait_for(ref, sem):
    pltpu.make_async_copy(ref, ref, sem).wait()


def send(src, dst, send_sem, recv_sem, where):
    pltpu.make_async_remote_copy(
        src_ref=src,
        dst_ref=dst,
        send_sem=send_sem,
        recv_sem=recv_sem,
        device_id=where,
        device_id_type=MESH,
    ).start()


def at(index, size):
    return pl.ds(pl.multiple_of(index * size, size), size)


def kernel(
    len_ref, q_hbm, k_hbm, v_hbm, g_hbm, bias_ref,
    gq, gkv, fin,
    q_ref, k_ref, v_ref, g_ref, tsend, kv, qd, bias_full, b2, kvt, qdt, s_ref, dp_ref, ph, dsh, acc, dqt, g32,
    psend, precv, gqsend, gkvsend, db, sib, rsend, red, redx, ysend, yrecv, fsend,
    kv_ss, kv_rs, qd_ss, qd_rs, fw_ss, fw_rs, b1_ss, b1_rs, b1_ls, b2_ss, b2_rs, by_ss, by_rs, b3_ss, b3_rs,
    p_ss, p_rs, gq_ss, gq_rs, gk_ss, gk_rs, a_ss, a_rs, r_ss, r_rs, f_ss, f_rs, y_ss, y_rs, in_ls,
):
    row = lax.axis_index("row")
    me = lax.axis_index("col")
    z = me % NZ
    yh = me // NZ
    chip = row // 2
    core = row % 2
    sibling = {"row": row + 1 - 2 * core}
    partner = {"col": (1 - yh) * NZ + z}
    others = [lax.rem(z + o, NZ) for o in range(1, NZ)]
    chips = [lax.rem(chip + o, NCHIP) for o in range(1, NCHIP)]

    def along_z(to):
        return {"col": yh * NZ + to}

    def along_row(to):
        return {"row": 2 * to + core}

    barrier = pltpu.get_barrier_semaphore()
    everyone = [along_z(to) for to in others] + [along_row(to) for to in chips] + [sibling, partner]
    everyone += [along_z(to) | sibling for to in others]
    for where in everyone:
        pl.semaphore_signal(barrier, inc=1, device_id=where, device_id_type=MESH)
    loads = [
        pltpu.make_async_copy(src, dst, in_ls.at[i])
        for i, (src, dst) in enumerate(((k_hbm, k_ref), (v_hbm, v_ref), (q_hbm, q_ref), (g_hbm, g_ref)))
    ]
    for load in loads:
        load.start()

    lane_block = lax.broadcasted_iota(jnp.int32, (BLK, 128), 1) // HD

    def lanes_from(parts):
        out = None
        for a, (x, b) in enumerate(parts):
            d = (a - b) % 4
            x = x if d == 0 else pltpu.roll(x, d * HD, 1)
            out = x if out is None else jnp.where(lane_block == a, x, out)
        return out

    def pack(u):
        for c in range(2):
            for kind, refs in enumerate(((k_ref, v_ref), (q_ref, g_ref))):
                arrays = [ref[c, 2 * u + e].astype(F32) for e in range(2) for ref in refs]
                for h in range(H):
                    tsend[u, kind, c * H + h] = lanes_from([(x, h) for x in arrays]).astype(BF16)
        kv[u, at(me, BLK), :] = tsend[u, 0, z]
        qd[u, at(z, BLK), :] = tsend[u, 1, z]

    def send_kv(u):
        for to in others:
            send(tsend.at[u, 0, to], kv.at[u, at(me, BLK)], kv_ss.at[u], kv_rs.at[u], along_z(to))

    def send_qd(u):
        for to in others:
            send(tsend.at[u, 1, to], qd.at[u, at(z, BLK)], qd_ss.at[u], qd_rs.at[u], along_z(to))

    def forward(u):
        wait_for(kv.at[u, pl.ds(0, BLK * (NZ - 1))], kv_rs.at[u])
        mine = kv.at[u, at(yh, HALF)]
        send(mine, mine, fw_ss.at[u], fw_rs.at[u], partner)

    ylo = chip // 4
    my_rows = pl.ds(pl.multiple_of(core * 32 + ylo * 16, 16), 16)
    their_rows = pl.ds(pl.multiple_of(core * 32 + (1 - ylo) * 16, 16), 16)
    my_lanes = at(chip % 4, 256)
    x_chips = [ylo * 4 + (chip + o) % 4 for o in range(1, 4)]
    y_chip = (1 - ylo) * 4 + chip % 4

    def bias_to_chips(jb):
        mine = bias_full.at[pl.ds(jb * 4, 4), my_rows, my_lanes]
        if jb == 1:
            send(mine, mine, by_ss.at[jb], by_rs.at[jb], along_row(y_chip))
        for to in x_chips if jb == 1 else chips:
            send(mine, mine, b2_ss.at[jb], b2_rs.at[jb], along_row(to))

    def bias_onward(jb):
        theirs = bias_full.at[pl.ds(jb * 4, 4), their_rows, my_lanes]
        wait_for(theirs, by_rs.at[jb])
        for to in x_chips:
            send(theirs, theirs, b2_ss.at[jb], b2_rs.at[jb], along_row(to))

    def bias_to_sibling(jb):
        wait_for(bias_full.at[pl.ds(0, 6 if jb else 7), :, pl.ds(0, 256)], b2_rs.at[jb])
        mine = bias_full.at[pl.ds(jb * 4, 4), at(core, 32)]
        send(mine, mine, b3_ss.at[jb], b3_rs.at[jb], sibling)

    for load in loads:
        load.wait()
    pack(0)
    pl.semaphore_wait(barrier, len(everyone))
    for to in others:
        send(
            bias_ref.at[to // H, to % H, my_rows, my_lanes],
            bias_full.at[z, my_rows, my_lanes],
            b1_ss,
            b1_rs,
            along_z(to),
        )
    own = pltpu.make_async_copy(
        bias_ref.at[z // H, z % H, my_rows, my_lanes], bias_full.at[z, my_rows, my_lanes], b1_ls
    )
    own.start()
    send_kv(0)
    send_qd(0)
    pack(1)
    own.wait()
    wait_for(bias_full.at[pl.ds(0, NZ - 1), pl.ds(0, 16), pl.ds(0, 256)], b1_rs)
    bias_to_chips(0)
    bias_to_chips(1)
    send_kv(1)
    pack(2)
    send_kv(2)
    send_qd(1)
    send_qd(2)
    forward(0)
    bias_onward(1)
    bias_to_sibling(0)
    n = len_ref[z // H]
    db[...] = jnp.zeros_like(db)

    def mask_bias(jb):
        col = lax.broadcasted_iota(jnp.int32, (R, SEQ), 1)
        for c in range(B // R):
            x = bias_full[jb * 4 + c // 4, pl.ds((c % 4) * R, R), :].astype(F32)
            b2[pl.ds(pl.multiple_of(jb * B + c * R, R), R), :] = jnp.where(col < n, x * LOG2E, -1e30)

    def prep(u):
        wait_for(qd.at[u, pl.ds(0, BLK * (NZ - 1))], qd_rs.at[u])
        x = qd[u]
        qdt[...] = x.T
        wait_for(kv.at[u, pl.ds(0, HALF)], fw_rs.at[u])
        x = kv[u]
        kvt[...] = x.T
        acc[...] = jnp.zeros_like(acc)
        dqt[...] = jnp.zeros_like(dqt)

    def tile(u, jb):
        j0 = pl.multiple_of(jb * B, B)
        rows = pl.ds(j0, B)
        for e in range(2):
            first, second = pl.ds(e * 64, HD), pl.ds(e * 64 + HD, HD)
            s_ref[e] = nn(qd[u, rows, first], kvt[first, :])
            dp_ref[e] = nn(qd[u, rows, second], kvt[second, :])
        for c in range(B // R):
            r = pl.ds(c * R, R)
            jr = pl.ds(pl.multiple_of(j0 + c * R, R), R)
            total = db[jr, :]
            for e in range(2):
                s = s_ref[e, r, :] * (SCALE * LOG2E) + b2[jr, :]
                m = jnp.max(s, axis=1, keepdims=True)
                w = jnp.exp2(s - m)
                dp = dp_ref[e, r, :]
                rl = 1.0 / jnp.sum(w, axis=1, keepdims=True)
                delta = jnp.sum(w * dp, axis=1, keepdims=True) * rl
                pr = w * rl
                ds = pr * (dp - delta)
                ph[e, r, :] = pr.astype(BF16)
                dsh[e, r, :] = ds.astype(BF16)
                total = total + ds
            db[jr, :] = total
        for e in range(2):
            dsv = dsh[e]
            first, second = pl.ds(e * 64, HD), pl.ds(e * 64 + HD, HD)
            dqt[pl.ds(e * HD, HD), rows] += lax.dot_general(
                kvt[first, :], dsv, (((1,), (1,)), ((), ())), preferred_element_type=F32
            )
            acc[first, :] += nn(qdt[first, rows], dsv)
            acc[second, :] += nn(qdt[second, rows], ph[e])

    def finish_kv(u):
        even = (lax.broadcasted_iota(jnp.int32, (SEQ, 128), 1) // HD) % 2 == 0
        g = acc[...].T
        g = jnp.where(even, g * SCALE, g).reshape(2 * NZ, BLK, 128)
        top, low = g[:, :32], g[:, 32:]
        lane = lax.broadcasted_iota(jnp.int32, top.shape, 2)
        g32[0] = jnp.where(lane < 64, top, pltpu.roll(low, 64, 2))
        g32[1] = jnp.where(lane < 64, pltpu.roll(top, 64, 2), low)
        for e in range(2):
            p = 2 * u + e
            psend[p] = g32[e, at(1 - yh, NZ)].astype(BF16)
            send(psend.at[p], precv.at[p], p_ss.at[p], p_rs.at[p], partner)

    def finish_q(u):
        x = jnp.concatenate([dqt[...] * SCALE, jnp.zeros_like(dqt)], axis=0).T
        x = x.reshape(NZ, BLK, 128)
        lane = lax.broadcasted_iota(jnp.int32, (NZ, 32, 128), 2)
        gqsend[u] = jnp.where(lane < 64, x[:, :32], pltpu.roll(x[:, 32:], 64, 2)).astype(BF16)
        gq[u, z] = gqsend[u, z]
        for to in others:
            send(gqsend.at[u, to], gq.at[u, z], gq_ss.at[u], gq_rs.at[u], along_z(to))

    def combine(p):
        wait_for(precv.at[p], p_rs.at[p])
        gkvsend[p] = (g32[p % 2, at(yh, NZ)] + precv[p].astype(F32)).astype(BF16)
        gkv[p, z] = gkvsend[p, z]
        for to in others:
            send(gkvsend.at[p, to], gkv.at[p, z], gk_ss.at[p], gk_rs.at[p], along_z(to))

    def db_to_sibling(jb):
        theirs = db.at[pl.ds(pl.multiple_of(jb * B + (1 - core) * SUB, SUB), SUB)]
        send(theirs, sib.at[jb], a_ss.at[jb], a_rs.at[jb], sibling)

    def db_over_row(jb):
        wait_for(sib.at[jb], a_rs.at[jb])
        mine = pl.ds(pl.multiple_of(jb * B + core * SUB, SUB), SUB)
        for o in range(NCHIP):
            lanes = pl.ds(o * 128, 128)
            rsend[jb, o] = (db[mine, lanes] + sib[jb, :, lanes]).astype(BF16)
        if jb == 0:
            redx[0, chip % 4] = rsend[0, chip]
            redx[1, chip % 4] = rsend[0, y_chip]
            for to in x_chips:
                send(rsend.at[0, to], redx.at[0, chip % 4], r_ss.at[0], r_rs.at[0], along_row(to))
                other = (1 - ylo) * 4 + to % 4
                send(rsend.at[0, other], redx.at[1, chip % 4], r_ss.at[0], r_rs.at[0], along_row(to))
        else:
            red[chip] = rsend[jb, chip]
            for to in chips:
                send(rsend.at[jb, to], red.at[chip], r_ss.at[jb], r_rs.at[jb], along_row(to))

    def db_cross():
        wait_for(rsend.at[0, pl.ds(0, 6)], r_rs.at[0])
        total = redx[1, 0].astype(F32)
        for o in range(1, 4):
            total = total + redx[1, o].astype(F32)
        ysend[...] = total
        send(ysend, yrecv, y_ss, y_rs, along_row(y_chip))

    def db_to_owner(jb):
        if jb == 0:
            wait_for(yrecv, y_rs)
            total = yrecv[...]
            for o in range(4):
                total = total + redx[0, o].astype(F32)
        else:
            wait_for(red.at[pl.ds(0, NCHIP - 1)], r_rs.at[jb])
            total = red[0].astype(F32)
            for o in range(1, NCHIP):
                total = total + red[o].astype(F32)
        lane = lax.broadcasted_iota(jnp.int32, (32, 128), 1)
        for e in range(2):
            to = jb * 4 + core * 2 + e
            top = total[e * BLK : e * BLK + 32]
            low = total[e * BLK + 32 : (e + 1) * BLK]
            fsend[jb * 4 + e * 2] = jnp.where(lane < 64, top, pltpu.roll(low, 64, 1))
            fsend[jb * 4 + e * 2 + 1] = jnp.where(lane < 64, pltpu.roll(top, 64, 1), low)
            for a in range(2):
                mine = (to == z) & (core == a)

                @pl.when(mine)
                def _():
                    fin[z] = fsend[jb * 4 + e * 2 + a]

                @pl.when(jnp.logical_not(mine))
                def _():
                    where = along_z(to) | {"row": 2 * chip + a}
                    send(fsend.at[jb * 4 + e * 2 + a], fin.at[z], f_ss, f_rs, where)

    @pl.loop(0, NP)
    def _(it):
        u = it // NJ
        jb = it % NJ

        @pl.when(jb == 0)
        def _():
            prep(u)

        @pl.when(u == 0)
        def _():
            @pl.when(jb == 0)
            def _():
                bias_to_sibling(1)

            wait_for(bias_full.at[pl.ds(0, 4), pl.ds(0, 32)], b3_rs.at[jb])
            mask_bias(jb)

        @pl.when(it < NU - 1)
        def _():
            forward(it + 1)

        tile(u, jb)

        @pl.when(u == NU - 1)
        def _():
            db_to_sibling(jb)

        @pl.when(it == NP - 1)
        def _():
            db_over_row(0)

        @pl.when((jb == 1) & (u > 0))
        def _():
            combine(2 * u - 2)
            combine(2 * u - 1)

        @pl.when(jb == 1)
        def _():
            finish_kv(u)
            finish_q(u)

    db_over_row(1)
    db_cross()
    combine(NP - 2)
    combine(NP - 1)
    db_to_owner(0)
    db_to_owner(1)
    wait_for(ysend, y_ss)
    owner = (z // 2) % 2 == core

    @pl.when(owner)
    def _():
        wait_for(fin.at[pl.ds(0, NZ - 1)], f_rs)
        wait_for(fsend.at[pl.ds(0, NZ - 1)], f_ss)

    @pl.when(jnp.logical_not(owner))
    def _():
        wait_for(fin, f_rs)
        wait_for(fsend, f_ss)

    wait_for(bias_full.at[pl.ds(0, NZ - 1), pl.ds(0, 16), pl.ds(0, 256)], b1_ss)
    for u in range(NU):
        wait_for(gq.at[u, pl.ds(0, NZ - 1)], gq_rs.at[u])
        wait_for(gq.at[u, pl.ds(0, NZ - 1)], gq_ss.at[u])
        wait_for(kv.at[u, pl.ds(0, BLK * (NZ - 1))], kv_ss.at[u])
        wait_for(qd.at[u, pl.ds(0, BLK * (NZ - 1))], qd_ss.at[u])
        wait_for(kv.at[u, pl.ds(0, HALF)], fw_ss.at[u])
    for p in range(NP):
        wait_for(gkv.at[p, pl.ds(0, NZ - 1)], gk_rs.at[p])
        wait_for(gkv.at[p, pl.ds(0, NZ - 1)], gk_ss.at[p])
        wait_for(psend.at[p], p_ss.at[p])
    for jb in range(NJ):
        wait_for(bias_full.at[pl.ds(0, 6 if jb else 7), :, pl.ds(0, 256)], b2_ss.at[jb])
        if jb == 1:
            wait_for(bias_full.at[pl.ds(0, 4), pl.ds(0, 16), pl.ds(0, 256)], by_ss.at[jb])
        wait_for(bias_full.at[pl.ds(0, 4), pl.ds(0, 32)], b3_ss.at[jb])
        wait_for(sib.at[jb], a_ss.at[jb])
        wait_for(rsend.at[jb, pl.ds(0, NCHIP - 1 if jb else 6)], r_ss.at[jb])


def unpack(gq, gkv, fin, dq_out, dk_out, dv_out, db_out):
    lane_block = lax.broadcasted_iota(jnp.int32, (BLK, 128), 1) // HD

    def lanes_from(parts):
        out = None
        for h, (x, b) in enumerate(parts):
            d = (h - b) % 4
            x = x if d == 0 else pltpu.roll(x, d * HD, 1)
            out = x if out is None else jnp.where(lane_block == h, x, out)
        return out

    def unfold(parts, lanes):
        parts = [x.astype(F32) for x in parts]
        return [jnp.concatenate([x, pltpu.roll(x, 128 - lanes, 1)], axis=0) for x in parts]

    for u in range(NU):
        folded = unfold([gq[u, h] for h in range(H)], 64)
        for e in range(2):
            pairs = unfold([gkv[2 * u + e, h] for h in range(H)], 64)
            dq_out[0, 2 * u + e] = lanes_from([(x, e) for x in folded])
            dk_out[0, 2 * u + e] = lanes_from([(x, 0) for x in pairs])
            dv_out[0, 2 * u + e] = lanes_from([(x, 1) for x in pairs])
    for h in range(H):
        x = fin[h]
        db_out[0, h, :32] = x[:, :64]
        db_out[0, h, 32:] = pltpu.roll(x, 64, 1)[:, :64]


def per_device(query, key, value, grad_out, pair_bias, crop_lengths):
    V = pltpu.VMEM
    D = pltpu.SemaphoreType.DMA
    vm = pl.BlockSpec(memory_space=V)
    gq, gkv, fin = pl.pallas_call(
        kernel,
        out_shape=(
            jax.ShapeDtypeStruct((NU, NZ, 32, 128), BF16),
            jax.ShapeDtypeStruct((NP, NZ, 32, 128), BF16),
            jax.ShapeDtypeStruct((NZ, 32, 128), F32),
        ),
        in_specs=[pl.BlockSpec(memory_space=pltpu.SMEM)] + [pl.BlockSpec(memory_space=pl.ANY)] * 5,
        out_specs=(vm, vm, vm),
        scratch_shapes=[V(query.shape, BF16)] * 4
        + [
            V((NU, 2, NZ, BLK, 128), BF16),
            V((NU, SEQ, 128), BF16),
            V((NU, HALF, 128), BF16),
            V((NZ, BLK, SEQ), BF16),
            V((HALF, SEQ), F32),
            V((128, SEQ), BF16),
            V((128, HALF), BF16),
            V((2, B, SEQ), F32),
            V((2, B, SEQ), F32),
            V((2, B, SEQ), BF16),
            V((2, B, SEQ), BF16),
            V((128, SEQ), F32),
            V((64, HALF), F32),
            V((2, 2 * NZ, 32, 128), F32),
            V((NP, NZ, 32, 128), BF16),
            V((NP, NZ, 32, 128), BF16),
            V((NU, NZ, 32, 128), BF16),
            V((NP, NZ, 32, 128), BF16),
            V((HALF, SEQ), F32),
            V((NJ, SUB, SEQ), F32),
            V((NJ, NCHIP, SUB, 128), BF16),
            V((NCHIP, SUB, 128), BF16),
            V((2, 4, SUB, 128), BF16),
            V((SUB, 128), F32),
            V((SUB, 128), F32),
            V((NZ, 32, 128), F32),
        ]
        + [D((NU,))] * 6
        + [D] * 3
        + [D((NJ,))] * 6
        + [D((NP,))] * 2
        + [D((NU,))] * 2
        + [D((NP,))] * 2
        + [D((NJ,))] * 4
        + [D] * 4
        + [D((4,))],
        compiler_params=pltpu.CompilerParams(
            vmem_limit_bytes=60 * 2**20, collective_id=0, has_side_effects=True
        ),
        cost_estimate=pl.CostEstimate(flops=8 * 10**9, bytes_accessed=4 * 10**6, transcendentals=3 * 2**20),
    )(crop_lengths, query, key, value, grad_out, pair_bias)
    grad = jax.ShapeDtypeStruct(query.shape, F32)
    spec = pl.BlockSpec((1, 6, BLK, 128), lambda c: (c, 0, 0, 0))
    return pl.pallas_call(
        unpack,
        grid=(2,),
        out_shape=(grad, grad, grad, jax.ShapeDtypeStruct((2, H, BLK, BLK), F32)),
        in_specs=[
            pl.BlockSpec((NU, H, 32, 128), lambda c: (0, c, 0, 0)),
            pl.BlockSpec((NP, H, 32, 128), lambda c: (0, c, 0, 0)),
            pl.BlockSpec((H, 32, 128), lambda c: (c, 0, 0)),
        ],
        out_specs=(spec, spec, spec, pl.BlockSpec((1, H, BLK, BLK), lambda c: (c, 0, 0, 0))),
    )(gq, gkv, fin)


def solution(mesh):
    spec = P(None, "row", "col", None)
    return jax.shard_map(
        per_device,
        mesh=mesh,
        in_specs=(spec, spec, spec, spec, P(None, None, "col", None), P()),
        out_specs=(spec, spec, spec, P(None, None, "col", "row")),
        check_vma=False,
    )
```

```python
import jax
import jax.numpy as jnp
from jax import lax
from jax.experimental import pallas as pl
from jax.experimental.pallas import tpu as pltpu
from jax.sharding import PartitionSpec as P

H = 4
HD = 32
SEQ = 1024
NZ = 8
BLK = 64
HALF = SEQ // 2
NU = 3
NP = 2 * NU
NCHIP = 8
B = 256
NJ = HALF // B
R = 16
SUB = B // 2
LOG2E = 1.4426950408889634
SCALE = HD**-0.5
F32 = jnp.float32
BF16 = jnp.bfloat16
MESH = pl.DeviceIdType.MESH


def nn(a, b):
    return lax.dot_general(a, b, (((1,), (0,)), ((), ())), preferred_element_type=F32)


def wait_for(ref, sem):
    pltpu.make_async_copy(ref, ref, sem).wait()


def send(src, dst, send_sem, recv_sem, where):
    pltpu.make_async_remote_copy(
        src_ref=src,
        dst_ref=dst,
        send_sem=send_sem,
        recv_sem=recv_sem,
        device_id=where,
        device_id_type=MESH,
    ).start()


def at(index, size):
    return pl.ds(pl.multiple_of(index * size, size), size)


def kernel(
    len_ref, q_hbm, k_hbm, v_hbm, g_hbm, bias_ref,
    gq, gkv, fin,
    q_ref, k_ref, v_ref, g_ref, tsend, kv, qd, bias_full, b2, kvt, qdt, s_ref, dp_ref, ph, dsh, acc, dqt, g32,
    psend, precv, gqsend, gkvsend, db, sib, rsend, red, redx, ysend, yrecv, fsend,
    kv_ss, kv_rs, qd_ss, qd_rs, fw_ss, fw_rs, b1_ss, b1_rs, b1_ls, b2_ss, b2_rs, by_ss, by_rs, b3_ss, b3_rs,
    p_ss, p_rs, gq_ss, gq_rs, gk_ss, gk_rs, a_ss, a_rs, r_ss, r_rs, f_ss, f_rs, y_ss, y_rs, in_ls,
):
    row = lax.axis_index("row")
    me = lax.axis_index("col")
    z = me % NZ
    yh = me // NZ
    chip = row // 2
    core = row % 2
    sibling = {"row": row + 1 - 2 * core}
    partner = {"col": (1 - yh) * NZ + z}
    others = [lax.rem(z + o, NZ) for o in range(1, NZ)]
    chips = [lax.rem(chip + o, NCHIP) for o in range(1, NCHIP)]

    def along_z(to):
        return {"col": yh * NZ + to}

    def along_row(to):
        return {"row": 2 * to + core}

    barrier = pltpu.get_barrier_semaphore()
    everyone = [along_z(to) for to in others] + [along_row(to) for to in chips] + [sibling, partner]
    everyone += [along_z(to) | sibling for to in others]
    for where in everyone:
        pl.semaphore_signal(barrier, inc=1, device_id=where, device_id_type=MESH)
    loads = [
        pltpu.make_async_copy(src, dst, in_ls.at[i])
        for i, (src, dst) in enumerate(((k_hbm, k_ref), (v_hbm, v_ref), (q_hbm, q_ref), (g_hbm, g_ref)))
    ]
    for load in loads:
        load.start()

    lane_block = lax.broadcasted_iota(jnp.int32, (BLK, 128), 1) // HD

    def lanes_from(parts):
        out = None
        for a, (x, b) in enumerate(parts):
            d = (a - b) % 4
            x = x if d == 0 else pltpu.roll(x, d * HD, 1)
            out = x if out is None else jnp.where(lane_block == a, x, out)
        return out

    def pack(u):
        for c in range(2):
            for kind, refs in enumerate(((k_ref, v_ref), (q_ref, g_ref))):
                arrays = [ref[c, 2 * u + e].astype(F32) for e in range(2) for ref in refs]
                for h in range(H):
                    tsend[u, kind, c * H + h] = lanes_from([(x, h) for x in arrays]).astype(BF16)
        kv[u, at(me, BLK), :] = tsend[u, 0, z]
        qd[u, at(z, BLK), :] = tsend[u, 1, z]

    def send_kv(u):
        for to in others:
            send(tsend.at[u, 0, to], kv.at[u, at(me, BLK)], kv_ss.at[u], kv_rs.at[u], along_z(to))

    def send_qd(u):
        for to in others:
            send(tsend.at[u, 1, to], qd.at[u, at(z, BLK)], qd_ss.at[u], qd_rs.at[u], along_z(to))

    def forward(u):
        wait_for(kv.at[u, pl.ds(0, BLK * (NZ - 1))], kv_rs.at[u])
        mine = kv.at[u, at(yh, HALF)]
        send(mine, mine, fw_ss.at[u], fw_rs.at[u], partner)

    ylo = chip // 4
    my_rows = pl.ds(pl.multiple_of(core * 32 + ylo * 16, 16), 16)
    their_rows = pl.ds(pl.multiple_of(core * 32 + (1 - ylo) * 16, 16), 16)
    my_lanes = at(chip % 4, 256)
    x_chips = [ylo * 4 + (chip + o) % 4 for o in range(1, 4)]
    y_chip = (1 - ylo) * 4 + chip % 4

    def bias_to_chips(jb):
        mine = bias_full.at[pl.ds(jb * 4, 4), my_rows, my_lanes]
        if jb == 1:
            send(mine, mine, by_ss.at[jb], by_rs.at[jb], along_row(y_chip))
        for to in x_chips if jb == 1 else chips:
            send(mine, mine, b2_ss.at[jb], b2_rs.at[jb], along_row(to))

    def bias_onward(jb):
        theirs = bias_full.at[pl.ds(jb * 4, 4), their_rows, my_lanes]
        wait_for(theirs, by_rs.at[jb])
        for to in x_chips:
            send(theirs, theirs, b2_ss.at[jb], b2_rs.at[jb], along_row(to))

    def bias_to_sibling(jb):
        wait_for(bias_full.at[pl.ds(0, 6 if jb else 7), :, pl.ds(0, 256)], b2_rs.at[jb])
        mine = bias_full.at[pl.ds(jb * 4, 4), at(core, 32)]
        send(mine, mine, b3_ss.at[jb], b3_rs.at[jb], sibling)

    for load in loads:
        load.wait()
    pack(0)
    pl.semaphore_wait(barrier, len(everyone))
    for to in others:
        send(
            bias_ref.at[to // H, to % H, my_rows, my_lanes],
            bias_full.at[z, my_rows, my_lanes],
            b1_ss,
            b1_rs,
            along_z(to),
        )
    own = pltpu.make_async_copy(
        bias_ref.at[z // H, z % H, my_rows, my_lanes], bias_full.at[z, my_rows, my_lanes], b1_ls
    )
    own.start()
    send_kv(0)
    send_qd(0)
    pack(1)
    own.wait()
    wait_for(bias_full.at[pl.ds(0, NZ - 1), pl.ds(0, 16), pl.ds(0, 256)], b1_rs)
    bias_to_chips(0)
    bias_to_chips(1)
    send_kv(1)
    pack(2)
    send_kv(2)
    send_qd(1)
    send_qd(2)
    forward(0)
    bias_onward(1)
    bias_to_sibling(0)
    n = len_ref[z // H]
    db[...] = jnp.zeros_like(db)

    def mask_bias(jb):
        col = lax.broadcasted_iota(jnp.int32, (R, SEQ), 1)
        for c in range(B // R):
            x = bias_full[jb * 4 + c // 4, pl.ds((c % 4) * R, R), :].astype(F32)
            b2[pl.ds(pl.multiple_of(jb * B + c * R, R), R), :] = jnp.where(col < n, x * LOG2E, -1e30)

    def prep(u):
        wait_for(qd.at[u, pl.ds(0, BLK * (NZ - 1))], qd_rs.at[u])
        x = qd[u]
        qdt[...] = x.T
        wait_for(kv.at[u, pl.ds(0, HALF)], fw_rs.at[u])
        x = kv[u]
        kvt[...] = x.T
        acc[...] = jnp.zeros_like(acc)
        dqt[...] = jnp.zeros_like(dqt)

    def tile(u, jb):
        j0 = pl.multiple_of(jb * B, B)
        rows = pl.ds(j0, B)
        for e in range(2):
            first, second = pl.ds(e * 64, HD), pl.ds(e * 64 + HD, HD)
            s_ref[e] = nn(qd[u, rows, first], kvt[first, :])
            dp_ref[e] = nn(qd[u, rows, second], kvt[second, :])
        for c in range(B // R):
            r = pl.ds(c * R, R)
            jr = pl.ds(pl.multiple_of(j0 + c * R, R), R)
            total = db[jr, :]
            for e in range(2):
                s = s_ref[e, r, :] * (SCALE * LOG2E) + b2[jr, :]
                m = jnp.max(s, axis=1, keepdims=True)
                w = jnp.exp2(s - m)
                dp = dp_ref[e, r, :]
                rl = 1.0 / jnp.sum(w, axis=1, keepdims=True)
                delta = jnp.sum(w * dp, axis=1, keepdims=True) * rl
                pr = w * rl
                ds = pr * (dp - delta)
                ph[e, r, :] = pr.astype(BF16)
                dsh[e, r, :] = ds.astype(BF16)
                total = total + ds
            db[jr, :] = total
        for e in range(2):
            dsv = dsh[e]
            first, second = pl.ds(e * 64, HD), pl.ds(e * 64 + HD, HD)
            dqt[pl.ds(e * HD, HD), rows] += lax.dot_general(
                kvt[first, :], dsv, (((1,), (1,)), ((), ())), preferred_element_type=F32
            )
            acc[first, :] += nn(qdt[first, rows], dsv)
            acc[second, :] += nn(qdt[second, rows], ph[e])

    def finish_kv(u):
        even = (lax.broadcasted_iota(jnp.int32, (SEQ, 128), 1) // HD) % 2 == 0
        g = acc[...].T
        g = jnp.where(even, g * SCALE, g).reshape(2 * NZ, BLK, 128)
        top, low = g[:, :32], g[:, 32:]
        lane = lax.broadcasted_iota(jnp.int32, top.shape, 2)
        g32[0] = jnp.where(lane < 64, top, pltpu.roll(low, 64, 2))
        g32[1] = jnp.where(lane < 64, pltpu.roll(top, 64, 2), low)
        for e in range(2):
            p = 2 * u + e
            psend[p] = g32[e, at(1 - yh, NZ)].astype(BF16)
            send(psend.at[p], precv.at[p], p_ss.at[p], p_rs.at[p], partner)

    def finish_q(u):
        x = jnp.concatenate([dqt[...] * SCALE, jnp.zeros_like(dqt)], axis=0).T
        x = x.reshape(NZ, BLK, 128)
        lane = lax.broadcasted_iota(jnp.int32, (NZ, 32, 128), 2)
        gqsend[u] = jnp.where(lane < 64, x[:, :32], pltpu.roll(x[:, 32:], 64, 2)).astype(BF16)
        gq[u, z] = gqsend[u, z]
        for to in others:
            send(gqsend.at[u, to], gq.at[u, z], gq_ss.at[u], gq_rs.at[u], along_z(to))

    def combine(p):
        wait_for(precv.at[p], p_rs.at[p])
        gkvsend[p] = (g32[p % 2, at(yh, NZ)] + precv[p].astype(F32)).astype(BF16)
        gkv[p, z] = gkvsend[p, z]
        for to in others:
            send(gkvsend.at[p, to], gkv.at[p, z], gk_ss.at[p], gk_rs.at[p], along_z(to))

    def db_to_sibling(jb):
        theirs = db.at[pl.ds(pl.multiple_of(jb * B + (1 - core) * SUB, SUB), SUB)]
        send(theirs, sib.at[jb], a_ss.at[jb], a_rs.at[jb], sibling)

    def db_over_row(jb):
        wait_for(sib.at[jb], a_rs.at[jb])
        mine = pl.ds(pl.multiple_of(jb * B + core * SUB, SUB), SUB)
        for o in range(NCHIP):
            lanes = pl.ds(o * 128, 128)
            rsend[jb, o] = (db[mine, lanes] + sib[jb, :, lanes]).astype(BF16)
        if jb == 0:
            redx[0, chip % 4] = rsend[0, chip]
            redx[1, chip % 4] = rsend[0, y_chip]
            for to in x_chips:
                send(rsend.at[0, to], redx.at[0, chip % 4], r_ss.at[0], r_rs.at[0], along_row(to))
                other = (1 - ylo) * 4 + to % 4
                send(rsend.at[0, other], redx.at[1, chip % 4], r_ss.at[0], r_rs.at[0], along_row(to))
        else:
            red[chip] = rsend[jb, chip]
            for to in chips:
                send(rsend.at[jb, to], red.at[chip], r_ss.at[jb], r_rs.at[jb], along_row(to))

    def db_cross():
        wait_for(rsend.at[0, pl.ds(0, 6)], r_rs.at[0])
        total = redx[1, 0].astype(F32)
        for o in range(1, 4):
            total = total + redx[1, o].astype(F32)
        ysend[...] = total
        send(ysend, yrecv, y_ss, y_rs, along_row(y_chip))

    def db_to_owner(jb):
        if jb == 0:
            wait_for(yrecv, y_rs)
            total = yrecv[...]
            for o in range(4):
                total = total + redx[0, o].astype(F32)
        else:
            wait_for(red.at[pl.ds(0, NCHIP - 1)], r_rs.at[jb])
            total = red[0].astype(F32)
            for o in range(1, NCHIP):
                total = total + red[o].astype(F32)
        lane = lax.broadcasted_iota(jnp.int32, (32, 128), 1)
        for e in range(2):
            to = jb * 4 + core * 2 + e
            top = total[e * BLK : e * BLK + 32]
            low = total[e * BLK + 32 : (e + 1) * BLK]
            fsend[jb * 4 + e * 2] = jnp.where(lane < 64, top, pltpu.roll(low, 64, 1))
            fsend[jb * 4 + e * 2 + 1] = jnp.where(lane < 64, pltpu.roll(top, 64, 1), low)
            for a in range(2):
                mine = (to == z) & (core == a)

                @pl.when(mine)
                def _():
                    fin[z] = fsend[jb * 4 + e * 2 + a]

                @pl.when(jnp.logical_not(mine))
                def _():
                    where = along_z(to) | {"row": 2 * chip + a}
                    send(fsend.at[jb * 4 + e * 2 + a], fin.at[z], f_ss, f_rs, where)

    @pl.loop(0, NP)
    def _(it):
        u = it // NJ
        jb = it % NJ

        @pl.when(jb == 0)
        def _():
            prep(u)

        @pl.when(it < NU - 1)
        def _():
            forward(it + 1)

        @pl.when(u == 0)
        def _():
            @pl.when(jb == 0)
            def _():
                bias_to_sibling(1)

            wait_for(bias_full.at[pl.ds(0, 4), pl.ds(0, 32)], b3_rs.at[jb])
            mask_bias(jb)

        tile(u, jb)

        @pl.when(u == NU - 1)
        def _():
            db_to_sibling(jb)

        @pl.when(it == NP - 1)
        def _():
            db_over_row(0)

        @pl.when((jb == 1) & (u > 0))
        def _():
            combine(2 * u - 2)
            combine(2 * u - 1)

        @pl.when(jb == 1)
        def _():
            finish_kv(u)
            finish_q(u)

    db_over_row(1)
    db_cross()
    combine(NP - 2)
    combine(NP - 1)
    db_to_owner(0)
    db_to_owner(1)
    wait_for(ysend, y_ss)
    owner = (z // 2) % 2 == core

    @pl.when(owner)
    def _():
        wait_for(fin.at[pl.ds(0, NZ - 1)], f_rs)
        wait_for(fsend.at[pl.ds(0, NZ - 1)], f_ss)

    @pl.when(jnp.logical_not(owner))
    def _():
        wait_for(fin, f_rs)
        wait_for(fsend, f_ss)

    wait_for(bias_full.at[pl.ds(0, NZ - 1), pl.ds(0, 16), pl.ds(0, 256)], b1_ss)
    for u in range(NU):
        wait_for(gq.at[u, pl.ds(0, NZ - 1)], gq_rs.at[u])
        wait_for(gq.at[u, pl.ds(0, NZ - 1)], gq_ss.at[u])
        wait_for(kv.at[u, pl.ds(0, BLK * (NZ - 1))], kv_ss.at[u])
        wait_for(qd.at[u, pl.ds(0, BLK * (NZ - 1))], qd_ss.at[u])
        wait_for(kv.at[u, pl.ds(0, HALF)], fw_ss.at[u])
    for p in range(NP):
        wait_for(gkv.at[p, pl.ds(0, NZ - 1)], gk_rs.at[p])
        wait_for(gkv.at[p, pl.ds(0, NZ - 1)], gk_ss.at[p])
        wait_for(psend.at[p], p_ss.at[p])
    for jb in range(NJ):
        wait_for(bias_full.at[pl.ds(0, 6 if jb else 7), :, pl.ds(0, 256)], b2_ss.at[jb])
        if jb == 1:
            wait_for(bias_full.at[pl.ds(0, 4), pl.ds(0, 16), pl.ds(0, 256)], by_ss.at[jb])
        wait_for(bias_full.at[pl.ds(0, 4), pl.ds(0, 32)], b3_ss.at[jb])
        wait_for(sib.at[jb], a_ss.at[jb])
        wait_for(rsend.at[jb, pl.ds(0, NCHIP - 1 if jb else 6)], r_ss.at[jb])


def unpack(gq, gkv, fin, dq_out, dk_out, dv_out, db_out):
    lane_block = lax.broadcasted_iota(jnp.int32, (BLK, 128), 1) // HD

    def lanes_from(parts):
        out = None
        for h, (x, b) in enumerate(parts):
            d = (h - b) % 4
            x = x if d == 0 else pltpu.roll(x, d * HD, 1)
            out = x if out is None else jnp.where(lane_block == h, x, out)
        return out

    def unfold(parts, lanes):
        parts = [x.astype(F32) for x in parts]
        return [jnp.concatenate([x, pltpu.roll(x, 128 - lanes, 1)], axis=0) for x in parts]

    for u in range(NU):
        folded = unfold([gq[u, h] for h in range(H)], 64)
        for e in range(2):
            pairs = unfold([gkv[2 * u + e, h] for h in range(H)], 64)
            dq_out[0, 2 * u + e] = lanes_from([(x, e) for x in folded])
            dk_out[0, 2 * u + e] = lanes_from([(x, 0) for x in pairs])
            dv_out[0, 2 * u + e] = lanes_from([(x, 1) for x in pairs])
    for h in range(H):
        x = fin[h]
        db_out[0, h, :32] = x[:, :64]
        db_out[0, h, 32:] = pltpu.roll(x, 64, 1)[:, :64]


def per_device(query, key, value, grad_out, pair_bias, crop_lengths):
    V = pltpu.VMEM
    D = pltpu.SemaphoreType.DMA
    vm = pl.BlockSpec(memory_space=V)
    gq, gkv, fin = pl.pallas_call(
        kernel,
        out_shape=(
            jax.ShapeDtypeStruct((NU, NZ, 32, 128), BF16),
            jax.ShapeDtypeStruct((NP, NZ, 32, 128), BF16),
            jax.ShapeDtypeStruct((NZ, 32, 128), F32),
        ),
        in_specs=[pl.BlockSpec(memory_space=pltpu.SMEM)] + [pl.BlockSpec(memory_space=pl.ANY)] * 5,
        out_specs=(vm, vm, vm),
        scratch_shapes=[V(query.shape, BF16)] * 4
        + [
            V((NU, 2, NZ, BLK, 128), BF16),
            V((NU, SEQ, 128), BF16),
            V((NU, HALF, 128), BF16),
            V((NZ, BLK, SEQ), BF16),
            V((HALF, SEQ), F32),
            V((128, SEQ), BF16),
            V((128, HALF), BF16),
            V((2, B, SEQ), F32),
            V((2, B, SEQ), F32),
            V((2, B, SEQ), BF16),
            V((2, B, SEQ), BF16),
            V((128, SEQ), F32),
            V((64, HALF), F32),
            V((2, 2 * NZ, 32, 128), F32),
            V((NP, NZ, 32, 128), BF16),
            V((NP, NZ, 32, 128), BF16),
            V((NU, NZ, 32, 128), BF16),
            V((NP, NZ, 32, 128), BF16),
            V((HALF, SEQ), F32),
            V((NJ, SUB, SEQ), F32),
            V((NJ, NCHIP, SUB, 128), BF16),
            V((NCHIP, SUB, 128), BF16),
            V((2, 4, SUB, 128), BF16),
            V((SUB, 128), F32),
            V((SUB, 128), F32),
            V((NZ, 32, 128), F32),
        ]
        + [D((NU,))] * 6
        + [D] * 3
        + [D((NJ,))] * 6
        + [D((NP,))] * 2
        + [D((NU,))] * 2
        + [D((NP,))] * 2
        + [D((NJ,))] * 4
        + [D] * 4
        + [D((4,))],
        compiler_params=pltpu.CompilerParams(
            vmem_limit_bytes=60 * 2**20, collective_id=0, has_side_effects=True
        ),
        cost_estimate=pl.CostEstimate(flops=8 * 10**9, bytes_accessed=4 * 10**6, transcendentals=3 * 2**20),
    )(crop_lengths, query, key, value, grad_out, pair_bias)
    grad = jax.ShapeDtypeStruct(query.shape, F32)
    spec = pl.BlockSpec((1, 6, BLK, 128), lambda c: (c, 0, 0, 0))
    return pl.pallas_call(
        unpack,
        grid=(2,),
        out_shape=(grad, grad, grad, jax.ShapeDtypeStruct((2, H, BLK, BLK), F32)),
        in_specs=[
            pl.BlockSpec((NU, H, 32, 128), lambda c: (0, c, 0, 0)),
            pl.BlockSpec((NP, H, 32, 128), lambda c: (0, c, 0, 0)),
            pl.BlockSpec((H, 32, 128), lambda c: (c, 0, 0)),
        ],
        out_specs=(spec, spec, spec, pl.BlockSpec((1, H, BLK, BLK), lambda c: (c, 0, 0, 0))),
    )(gq, gkv, fin)


def solution(mesh):
    spec = P(None, "row", "col", None)
    return jax.shard_map(
        per_device,
        mesh=mesh,
        in_specs=(spec, spec, spec, spec, P(None, None, "col", None), P()),
        out_specs=(spec, spec, spec, P(None, None, "col", "row")),
        check_vma=False,
    )
```
